512 devices in a mesh: space: 64 (over x, z), tm: 8 (over y, core).
Axes of the slice: x: 4, y: 4, z: 16, core: 2. Of those that a mesh axis runs over, the one named last changes fastest.
Arguments:
- trajectory: float32 [64, 6, 65536], P('tm', None, 'space'), as said below
- counts: int32 [64, 64], P('space'), may hold values from 0 to 24, as said below
- particle_ids: int32 [65536], P('space'), may hold values from 0 to 196607, as said below
Outputs:
- coefficients: float32 [64, 6, 98304], P('tm', None, 'space')
- owned_ids: int32 [98304], P('space')
The draws below stay inside these ranges and needn't reach their ends.
Inputs may be any that keep to these rules, and one draw needn't show every extreme that they name: `counts`: each row sums to 1024. Column pairs drawn from the seed split every region's rows: one owner of each pair gets 1024 // 64 plus some amount, the other that much less; one owner receives exactly 24 from every region. `particle_ids`: within a region's block the rows are grouped by owner in rising order; a row sent to owner o has an ID in [o * 3072, (o + 1) * 3072), and IDs rise within each region's block. `trajectory`: positions lie in [0, 4); velocity components within 0.3 of magnitude apart from small noise; the position change between snapshots stays far below half the box.
All inputs are finite; a program needn't handle non-finite values.
Results may differ from the reference program's by a relative error of at most 0.0003.
Values sent between devices are 32-bit elements; how exact they have to be, the bound alone decides.
A program may use at most 64 MiB of HBM per device.

```python
import jax
import jax.numpy as jnp
from jax import lax

ROWS_DEV = 1024
LEVELS = 3
REGIONS = 64
SNAPS = 64
PARTICLES = 65536
CAP = 24
SLOTS = 98304
ID_SPAN = 3072


def region_counts(key):
    mean_rows = ROWS_DEV // REGIONS
    half_rows = mean_rows // 2
    pairs = REGIONS // 2
    order = jax.random.permutation(jax.random.fold_in(key, 11), REGIONS)
    moved = jax.random.randint(jax.random.fold_in(key, 12), (REGIONS, pairs), 0, half_rows + 1)
    moved = moved.at[:, 0].set(half_rows)
    heavy = order[0::2]
    light = order[1::2]
    table = jnp.zeros((REGIONS, REGIONS), jnp.int32) + mean_rows
    table = table.at[:, heavy].add(moved).at[:, light].add(-moved)
    return table.astype(jnp.int32)


def draw_counts(key, part):
    return region_counts(key)


def draw_particle_ids(key, part):
    table = region_counts(key)
    key = jax.random.fold_in(key, 5)
    ends = jnp.cumsum(table, axis=1)
    starts = ends - table
    position = jnp.arange(ROWS_DEV, dtype=jnp.int32)
    owner = jnp.sum((position[None, :, None] >= ends[:, None, :]).astype(jnp.int32), axis=2)
    start_of = jnp.sum(jnp.where(owner[:, :, None] == jnp.arange(REGIONS, dtype=jnp.int32)[None, None, :], starts[:, None, :], 0), axis=2)
    within = position[None, :] - start_of
    region = jnp.arange(REGIONS, dtype=jnp.int32)[:, None]
    parity = jax.random.randint(key, (REGIONS, ROWS_DEV), 0, 2)
    ids = owner * ID_SPAN + 2 * (region * CAP + within) + parity
    return ids.reshape(PARTICLES).astype(jnp.int32)


def draw_trajectory(key, part):
    key = jax.random.fold_in(key, 7)
    base = jax.random.uniform(jax.random.fold_in(key, 1), (1, 3, PARTICLES), jnp.float32, 0.0, 4.0)
    drift = jax.random.uniform(jax.random.fold_in(key, 2), (1, 3, PARTICLES), jnp.float32, -0.15, 0.15)
    times = jnp.arange(SNAPS, dtype=jnp.float32).reshape(SNAPS, 1, 1)
    jitter = 0.04 * jax.random.normal(jax.random.fold_in(key, 3), (SNAPS, 3, PARTICLES), jnp.float32)
    wobble = 0.03 * jax.random.normal(jax.random.fold_in(key, 4), (SNAPS, 3, PARTICLES), jnp.float32)
    position = jnp.mod(base + drift * times + jitter, 4.0)
    velocity = drift + wobble
    return jnp.concatenate([position, velocity], axis=1).astype(jnp.float32)


def setup_inputs(seed: int = 0) -> dict:
    splits = jax.random.split(jax.random.key(seed), 4)
    return {
        "trajectory": draw_trajectory(jax.random.fold_in(splits[3], 71), 0),
        "counts": draw_counts(jax.random.fold_in(splits[3], 71), 0),
        "particle_ids": draw_particle_ids(jax.random.fold_in(splits[3], 71), 0),
    }


box_length = 4.0


def wrapped(delta):
    return delta - box_length * jnp.floor(delta / box_length + 0.5)


def hermite(start, finish, spacing):
    shift_pos = wrapped(finish[:, :3] - start[:, :3])
    guess_pos = start[:, :3] + 0.5 * shift_pos + 0.25 * spacing * (start[:, 3:] - finish[:, 3:])
    guess_vel = 0.75 * shift_pos / spacing - 0.25 * (start[:, 3:] + finish[:, 3:])
    return jnp.concatenate([guess_pos, guess_vel], axis=1)


def extrapolate(start, spacing):
    return jnp.concatenate([start[:, :3] + spacing * start[:, 3:], start[:, 3:]], axis=1)


def residue(odds, guess):
    return jnp.concatenate([wrapped(odds[:, :3] - guess[:, :3]), odds[:, 3:] - guess[:, 3:]], axis=1)


def lift_whole(block):
    for level in range(LEVELS):
        step = 2 ** level
        spacing = float(step)
        evens = block[0::2 * step]
        odds = block[step::2 * step]
        guess = jnp.concatenate([hermite(evens[:-1], evens[1:], spacing), extrapolate(evens[-1:], spacing)], axis=0)
        detail = residue(odds, guess)
        lefts = jnp.concatenate([detail[:1], detail[:-1]], axis=0)
        evens = evens + 0.25 * (lefts + detail)
        block = block.at[0::2 * step].set(evens).at[step::2 * step].set(detail)
    return block


def reference(trajectory, counts, particle_ids):
    offsets = (jnp.cumsum(counts, axis=1) - counts).astype(jnp.int32)
    slot = jnp.arange(REGIONS * CAP, dtype=jnp.int32)
    region = slot // CAP
    within = slot % CAP

    def owner_block(owner):
        count_col = lax.dynamic_slice_in_dim(counts, owner, 1, 1)[:, 0]
        offset_col = lax.dynamic_slice_in_dim(offsets, owner, 1, 1)[:, 0]
        live = within < jnp.repeat(count_col, CAP, total_repeat_length=REGIONS * CAP)
        source = region * ROWS_DEV + jnp.repeat(offset_col, CAP, total_repeat_length=REGIONS * CAP) + within
        source = jnp.where(live, source, 0).astype(jnp.int32)
        gathered = jnp.where(live[None, None, :], jnp.take(trajectory, source, axis=2), jnp.float32(0.0))
        tags = jnp.where(live, jnp.take(particle_ids, source), -1).astype(jnp.int32)
        return lift_whole(gathered), tags

    lifted, tags = lax.map(owner_block, jnp.arange(REGIONS, dtype=jnp.int32))
    coefficients = jnp.transpose(lifted, (1, 2, 0, 3)).reshape(SNAPS, 6, SLOTS)
    return coefficients, tags.reshape(SLOTS)
```

```python
import functools

import jax
import jax.numpy as jnp
from jax import lax
from jax.experimental import pallas as pl
from jax.experimental.pallas import tpu as pltpu
from jax.sharding import PartitionSpec as P

MESH = pl.DeviceIdType.MESH
NX = 4
NZ = 16
NT = 8
CAP = 24
ROWS = 1024
LANES = 128
WIDE = NZ * CAP
CHUNK = 256
REACH = 4
NEAR = (4, 12, 3, 13, 2, 14, 1, 15)
FAR = (8, 7, 9, 6, 10, 5, 11)
FAR_FIRST = FAR + NEAR
TILES1 = 2
TILES2 = 3


def wrapped(delta):
    return delta - 4.0 * jnp.floor(delta * 0.25 + 0.5)


def detail_of(start, odd, finish, h, final=None):
    (xa, va), (xo, vo), (xb, vb) = start, odd, finish
    shift = wrapped(xb - xa)
    guess_x = xa + 0.5 * shift + (0.25 * h) * (va - vb)
    guess_v = (0.75 / h) * shift - 0.25 * (va + vb)
    if final is not None:
        guess_x = jnp.where(final, xa + h * va, guess_x)
        guess_v = jnp.where(final, va, guess_v)
    return wrapped(xo - guess_x), vo - guess_v


def updated(even, left, right):
    return tuple(e + 0.25 * (a + b) for e, a, b in zip(even, left, right))


def chosen(flag, a, b):
    return tuple(jnp.where(flag, p, q) for p, q in zip(a, b))


def kernel(
    counts_hbm, ids_hbm, traj, coef, oid,
    counts, ids, x, s1, s2, to_left, to_right, from_right, from_left, edge, edge_in,
    zs1, zs2, zr1, zr2, tail, u1, u2, a1, a2, aid, offs,
    load_sem, far_sem, halo_s, halo_r, z_s1, z_r1, z_s2, z_r2, x_s, x_r,
):
    me = lax.axis_index("space")
    mx, mz = me // NZ, me % NZ
    mt = lax.axis_index("tm")
    first, final = mt == 0, mt == NT - 1
    left, right = (mt + NT - 1) % NT, (mt + 1) % NT

    def z_peer(k):
        z = (mz + k) % NZ
        return z, {"space": mx * NZ + z}

    def x_peer(k):
        xp = (mx + k) % NX
        return xp, {"space": xp * NZ + mz}

    barrier = pltpu.get_barrier_semaphore()
    peers = [z_peer(k)[1] for k in NEAR] + [x_peer(k)[1] for k in range(1, NX)]
    peers += [{"tm": left}, {"tm": right}]
    for peer in peers:
        pl.semaphore_signal(barrier, inc=1, device_id=peer, device_id_type=MESH)

    loads = [
        pltpu.make_async_copy(counts_hbm, counts, load_sem.at[0]),
        pltpu.make_async_copy(traj, x, load_sem.at[1]),
        pltpu.make_async_copy(ids_hbm, ids, load_sem.at[2]),
    ]
    for load in loads:
        load.start()
    loads[0].wait()
    total = jnp.int32(0)
    for o in range(NX * NZ):
        offs[o] = total
        total = total + counts[0, o]
    loads[1].wait()
    loads[2].wait()

    def snap(i, lanes):
        return x[0:3, i, lanes], x[3:6, i, lanes]

    def pair(ref, i, lanes):
        return ref[6 * i : 6 * i + 3, lanes], ref[6 * i + 3 : 6 * i + 6, lanes]

    def put(ref, i, lanes, value):
        ref[6 * i : 6 * i + 3, lanes], ref[6 * i + 3 : 6 * i + 6, lanes] = value

    for c in range(ROWS // CHUNK):
        lanes = slice(c * CHUNK, (c + 1) * CHUNK)
        p = [snap(i, lanes) for i in range(8)]
        d1 = detail_of(p[0], p[1], p[2], 1.0)
        d3 = detail_of(p[2], p[3], p[4], 1.0)
        d5 = detail_of(p[4], p[5], p[6], 1.0)
        e2 = updated(p[2], d1, d3)
        e4 = updated(p[4], d3, d5)
        for i, v in enumerate((d1, d3, d5)):
            put(s1, i, lanes, v)
        s1[18:20, lanes] = d5[1][1:3]
        s1[20:24, lanes] = jnp.zeros((4, CHUNK), jnp.float32)
        for i, v in enumerate((p[0], d1, e2, e4)):
            put(to_left, i, lanes, v)
        for i, v in enumerate((e4, d5, p[6], p[7])):
            put(to_right, i, lanes, v)
        s2[30:31, lanes] = (ids[0:1, lanes] + 1).astype(jnp.float32)
        s2[31:32, lanes] = jnp.zeros((1, CHUNK), jnp.float32)

    lane = lax.broadcasted_iota(jnp.int32, (8, LANES), 1)
    row = lax.broadcasted_iota(jnp.int32, (8, LANES), 0)

    def window(o):
        owners = NX * NZ
        low = max(0, ROWS - CAP * (owners - o))
        high = min(CAP * o, ROWS - 1)
        tiles = range(low // LANES, min(high + CAP - 1, ROWS - 1) // LANES + 1)
        off = offs[o]
        tile = (off >> 7) + (lane < (off & (LANES - 1))).astype(jnp.int32)
        return tiles, tile, off, counts[0, o]

    def taken(src, strip, tiles, tile, index):
        rows = slice(8 * strip, 8 * strip + 8)
        block = src[rows, tiles[0] * LANES : (tiles[0] + 1) * LANES]
        for t in tiles[1:]:
            block = jnp.where(tile == t, src[rows, t * LANES : (t + 1) * LANES], block)
        return jnp.take_along_axis(block, index, axis=1, mode="promise_in_bounds")

    def pack(src, full, z, last_apart):
        out = [jnp.zeros((8, LANES), jnp.float32) for _ in range(full)]
        apart = []
        for xp in range(NX):
            tiles, tile, off, count = window(xp * NZ + z)
            begin = xp * CAP
            index = (lane + (off - begin)) & (LANES - 1)
            live = (lane >= begin) & (lane < begin + count)
            for strip in range(full):
                out[strip] = jnp.where(live, taken(src, strip, tiles, tile, index), out[strip])
            if last_apart:
                begin = NX * CAP
                index = (lane + (off - begin)) & (LANES - 1)
                live = (lane >= begin) & (lane < begin + count)
                apart.append(jnp.where(live, taken(src, full, tiles, tile, index), 0.0))
        return out, apart

    spare = lane >= NX * CAP
    for z in range(NZ):
        out, apart = pack(s1, TILES1, z, True)
        for i in range(TILES1):
            zs1[z, 8 * i : 8 * i + 8, :] = jnp.where(
                spare, jnp.where(row < 2, apart[i], apart[i + 2]), out[i]
            )

    def remote(src, dst, send, recv, peer):
        return pltpu.make_async_remote_copy(
            src_ref=src, dst_ref=dst, send_sem=send, recv_sem=recv, device_id=peer, device_id_type=MESH
        )

    halos = [
        remote(to_left, from_right, halo_s.at[0], halo_r.at[0], {"tm": left}),
        remote(to_right, from_left, halo_s.at[1], halo_r.at[1], {"tm": right}),
        remote(edge, edge_in, halo_s.at[2], halo_r.at[2], {"tm": right}),
    ]

    def z_send(k, zs, zr, send, recv):
        z, peer = z_peer(k)
        return remote(zs.at[z], zr.at[mz], send.at[z], recv.at[mz], peer)

    def z_arrival(k, zs, zr, send, recv):
        z, peer = z_peer(k)
        return remote(zs.at[z], zr.at[z], send.at[z], recv.at[z], peer)

    pl.semaphore_wait(barrier, len(peers))
    for k in (REACH, NZ - REACH):
        pl.semaphore_signal(far_sem, inc=1, device_id=z_peer(k)[1], device_id_type=MESH)
    halos[0].start()
    halos[1].start()
    for k in NEAR:
        z_send(k, zs1, zr1, z_s1, z_r1).start()
    pl.semaphore_wait(far_sem, 2)
    for k in FAR:
        z_send(k, zs1, zr1, z_s1, z_r1).start()
    zr1[mz] = zs1[mz]

    halos[0].wait_recv()
    halos[1].wait_recv()

    for c in range(ROWS // CHUNK):
        lanes = slice(c * CHUNK, (c + 1) * CHUNK)
        x0, d1, e2, e4 = (pair(to_left, i, lanes) for i in range(4))
        d5, x6, x7 = (pair(to_right, i, lanes) for i in range(1, 4))
        x8, d9, e10, e12 = (pair(from_right, i, lanes) for i in range(4))
        em4, dm3, xm2, xm1 = (pair(from_left, i, lanes) for i in range(4))
        dm1 = detail_of(xm2, xm1, x0, 1.0)
        e0 = updated(x0, chosen(first, d1, dm1), d1)
        d7 = detail_of(x6, x7, x8, 1.0, final)
        e6 = updated(x6, d5, d7)
        e8 = updated(x8, d7, d9)
        em2 = updated(xm2, dm3, dm1)
        dm2 = detail_of(em4, em2, e0, 2.0)
        d2 = detail_of(e0, e2, e4, 2.0)
        d6 = detail_of(e4, e6, e8, 2.0, final)
        d10 = detail_of(e8, e10, e12, 2.0)
        f0 = updated(e0, chosen(first, d2, dm2), d2)
        f4 = updated(e4, d2, d6)
        f8 = updated(e8, d6, d10)
        d4 = detail_of(f0, f4, f8, 4.0, final)
        for i, v in enumerate((f0, d2, d4, d6, d7)):
            put(s2, i, lanes, v)
        put(edge, 0, lanes, d4)

    halos[2].start()
    halos[2].wait_recv()

    d4 = edge[...]
    before = jnp.where(first, d4, edge_in[...])
    s2[0:6, :] = s2[0:6, :] + 0.25 * (before + d4)

    for z in range(NZ):
        out, _ = pack(s2, TILES2 + 1, z, False)
        for i in range(TILES2):
            moved = pltpu.roll(out[TILES2], NX * CAP - 32 * i, 1)
            zs2[z, 8 * i : 8 * i + 8, :] = jnp.where(spare, moved, out[i])
    for k in FAR_FIRST:
        z_send(k, zs2, zr2, z_s2, z_r2).start()
    zr2[mz] = zs2[mz]

    def placed(u, strip, part):
        rows = slice(8 * strip, 8 * strip + 8)
        for xp in range(NX):
            tiles = [None] * (WIDE // LANES)
            for z in range(NZ):
                block, begin = part(z, xp)
                turn = (z * CAP - begin) % LANES
                turned = pltpu.roll(block, turn, 1) if turn else block
                for t in range(WIDE // LANES):
                    low, high = z * CAP - t * LANES, (z + 1) * CAP - t * LANES
                    if high > 0 and low < LANES:
                        old = tiles[t]
                        tiles[t] = turned if old is None else jnp.where(lane >= low, turned, old)
            for t in range(WIDE // LANES):
                u[xp, rows, t * LANES : (t + 1) * LANES] = tiles[t]

    own = pl.ds(pl.multiple_of(mx * WIDE, LANES), WIDE)

    def lanes_from(xp):
        return pl.ds(pl.multiple_of(xp * WIDE, LANES), WIDE)

    def parts(xp, here):
        return (
            (a1.at[xp], coef.at[0:3, 1, :, here]),
            (a2.at[xp, 0:4], coef.at[0:4, 0, :, here]),
            (a2.at[xp, 4], coef.at[3, 1, :, here]),
            (aid.at[xp], oid.at[:, here]),
        )

    def to_owner(k, i):
        xp, peer = x_peer(k)
        src, dst = parts(xp, own)[i]
        return remote(src, dst, x_s.at[k, i], x_r.at[k, i], peer)

    def from_region(k, i):
        xp, peer = x_peer(NX - k)
        src, dst = parts(xp, lanes_from(xp))[i]
        return remote(src, dst, x_s.at[k, i], x_r.at[k, i], peer)

    for k in FAR_FIRST:
        z_arrival(k, zs1, zr1, z_s1, z_r1).wait_recv()
    for strip in range(TILES1):
        placed(u1, strip, lambda z, xp: (zr1[z, 8 * strip : 8 * strip + 8, :], xp * CAP))
    placed(u1, TILES1, lambda z, xp: (zr1[z, 8 * (xp % 2) : 8 * (xp % 2) + 8, :], NX * CAP))
    for xp in range(NX):
        a1[xp, 0] = u1[xp, 0:6, :]
        a1[xp, 1] = u1[xp, 6:12, :]
        a1[xp, 2, 0:4] = u1[xp, 12:16, :]
        last = 16 + 2 * (xp // 2)
        a1[xp, 2, 4:6] = u1[xp, last : last + 2, :]
    for k in (2, 1, 3):
        to_owner(k, 0).start()
    coef[0:3, 1, :, own] = a1[mx]

    for k in FAR_FIRST:
        z_arrival(k, zs2, zr2, z_s2, z_r2).wait_recv()
    for strip in range(TILES2):
        placed(u2, strip, lambda z, xp: (zr2[z, 8 * strip : 8 * strip + 8, :], xp * CAP))
    for z in range(NZ):
        whole = pltpu.roll(zr2[z, 0:8, :], 32, 1)
        whole = jnp.where(lane < 32, whole, pltpu.roll(zr2[z, 8:16, :], 64, 1))
        last = jnp.where(lane < 64, whole, pltpu.roll(zr2[z, 16:24, :], 96, 1))
        tail[z] = last
    placed(u2, TILES2, lambda z, xp: (tail[z], xp * CAP))
    for xp in range(NX):
        for i in range(5):
            a2[xp, i] = u2[xp, 6 * i : 6 * i + 6, :]
        aid[xp] = u2[xp, 30:31, :].astype(jnp.int32) - 1
    for i in (1, 2, 3):
        for k in (2, 1, 3):
            to_owner(k, i).start()
    coef[0:4, 0, :, own] = a2[mx, 0:4]
    coef[3, 1, :, own] = a2[mx, 4]
    oid[:, own] = aid[mx]

    for k in (2, 1, 3):
        for i in range(4):
            from_region(k, i).wait_recv()
    for halo in halos:
        halo.wait_send()
    for k in FAR_FIRST:
        z_send(k, zs1, zr1, z_s1, z_r1).wait_send()
        z_send(k, zs2, zr2, z_s2, z_r2).wait_send()
    for k in (2, 1, 3):
        for i in range(4):
            to_owner(k, i).wait_send()


def per_device(trajectory, counts, particle_ids):
    f32, i32 = jnp.float32, jnp.int32
    vmem = lambda *shape: pltpu.VMEM(shape, f32)
    dma = pltpu.SemaphoreType.DMA
    slots = NX * WIDE
    coefficients, owned = pl.pallas_call(
        kernel,
        out_shape=(
            jax.ShapeDtypeStruct((4, 2, 6, slots), f32),
            jax.ShapeDtypeStruct((1, slots), i32),
        ),
        in_specs=[pl.BlockSpec(memory_space=pltpu.HBM)] * 3,
        out_specs=(pl.BlockSpec(memory_space=pltpu.VMEM), pl.BlockSpec(memory_space=pltpu.VMEM)),
        scratch_shapes=[
            pltpu.SMEM((1, NX * NZ), i32), pltpu.VMEM((1, ROWS), i32), vmem(6, 8, ROWS),
            vmem(24, ROWS), vmem(32, ROWS),
            vmem(24, ROWS), vmem(24, ROWS), vmem(24, ROWS), vmem(24, ROWS),
            vmem(6, ROWS), vmem(6, ROWS),
            vmem(NZ, 8 * TILES1, LANES), vmem(NZ, 8 * TILES2, LANES),
            vmem(NZ, 8 * TILES1, LANES), vmem(NZ, 8 * TILES2, LANES), vmem(NZ, 8, LANES),
            vmem(NX, 24, WIDE), vmem(NX, 32, WIDE),
            vmem(NX, 3, 6, WIDE), vmem(NX, 5, 6, WIDE),
            pltpu.VMEM((NX, 1, WIDE), i32), pltpu.SMEM((NX * NZ,), i32),
            dma((3,)), pltpu.SemaphoreType.REGULAR, dma((3,)), dma((3,)),
            dma((NZ,)), dma((NZ,)), dma((NZ,)), dma((NZ,)), dma((NX, 4)), dma((NX, 4)),
        ],
        compiler_params=pltpu.CompilerParams(
            collective_id=0, has_side_effects=True, vmem_limit_bytes=60 * 2**20
        ),
        name="regroup_and_lift",
    )(counts, particle_ids.reshape(1, ROWS), trajectory.transpose(1, 0, 2))
    return coefficients.reshape(8, 6, slots), owned.reshape(slots)


def solution(mesh):
    return jax.shard_map(
        per_device,
        mesh=mesh,
        in_specs=(P("tm", None, "space"), P("space", None), P("space")),
        out_specs=(P("tm", None, "space"), P("space")),
        check_vma=False,
    )
```

```python
import functools

import jax
import jax.numpy as jnp
from jax import lax
from jax.experimental import pallas as pl
from jax.experimental.pallas import tpu as pltpu
from jax.sharding import PartitionSpec as P

MESH = pl.DeviceIdType.MESH
NX = 4
NZ = 16
NT = 8
CAP = 24
ROWS = 1024
LANES = 128
SLOT_TILES = NX * NZ * CAP // LANES
WIDE = NZ * CAP
X_TILES = WIDE // LANES
CHUNK = 256
X_ORDER = (2, 1, 3)
REACH = 4
NEAR = (4, 12, 3, 13, 2, 14, 1, 15)
FAR = (5, 11, 6, 10, 7, 9, 8)
FAR_FIRST = (8, 7, 9, 6, 10, 5, 11) + NEAR
SPAN = NX * CAP
PHASES = ((24, 2), (24, 2), (8, 1))


def wrapped(delta):
    return delta - 4.0 * jnp.floor(delta * 0.25 + 0.5)


def detail_of(start, odd, finish, h, final=None):
    (xa, va), (xo, vo), (xb, vb) = start, odd, finish
    shift = wrapped(xb - xa)
    guess_x = xa + 0.5 * shift + (0.25 * h) * (va - vb)
    guess_v = (0.75 / h) * shift - 0.25 * (va + vb)
    if final is not None:
        guess_x = jnp.where(final, xa + h * va, guess_x)
        guess_v = jnp.where(final, va, guess_v)
    return wrapped(xo - guess_x), vo - guess_v


def updated(even, left, right):
    return tuple(e + 0.25 * (a + b) for e, a, b in zip(even, left, right))


def chosen(flag, a, b):
    return tuple(jnp.where(flag, p, q) for p, q in zip(a, b))


def kernel(
    counts_hbm, ids_hbm, traj, coef, oid,
    counts, ids, x, s0, s1, s2, to_left, to_right, from_right, from_left, edge, edge_in,
    index, place, offs, xs0, xs1, xs2, xr0, xr1, xr2, zs0, zs1, zs2, zr0, zr1, zr2, tail, u0, u1, w0,
    load_sem, far_sem, halo_s, halo_r, z_s, z_r, x_s, x_r,
):
    me = lax.axis_index("space")
    mx, mz = me // NZ, me % NZ
    mt = lax.axis_index("tm")
    first, final = mt == 0, mt == NT - 1
    left, right = (mt + NT - 1) % NT, (mt + 1) % NT
    rows_of, xs, xr = (s0, s1, s2), (xs0, xs1, xs2), (xr0, xr1, xr2)
    zs, zr = (zs0, zs1, zs2), (zr0, zr1, zr2)

    def z_peer(k):
        z = (mz + k) % NZ
        return z, {"space": mx * NZ + z}

    def x_peer(k):
        xp = (mx + k) % NX
        return xp, {"space": xp * NZ + mz}

    barrier = pltpu.get_barrier_semaphore()
    peers = [z_peer(k)[1] for k in NEAR] + [x_peer(k)[1] for k in X_ORDER]
    peers += [{"tm": left}, {"tm": right}]
    for peer in peers:
        pl.semaphore_signal(barrier, inc=1, device_id=peer, device_id_type=MESH)

    loads = [
        pltpu.make_async_copy(counts_hbm, counts, load_sem.at[0]),
        pltpu.make_async_copy(traj, x, load_sem.at[1]),
        pltpu.make_async_copy(ids_hbm, ids, load_sem.at[2]),
    ]
    for load in loads:
        load.start()
    loads[0].wait()
    total = jnp.int32(0)
    for o in range(NX * NZ):
        offs[o] = total
        total = total + counts[0, o]

    lane = lax.broadcasted_iota(jnp.int32, (8, LANES), 1)
    row = lax.broadcasted_iota(jnp.int32, (8, LANES), 0)
    spare = lane >= SPAN

    for t in range(SLOT_TILES):
        base = t * LANES
        o0 = base // CAP
        shift, end = None, None
        for o in range(o0, (base + LANES - 1) // CAP + 1):
            begin = o * CAP - base
            shift_o, end_o = offs[o] - begin, begin + counts[0, o]
            if shift is None:
                shift, end = jnp.full((8, LANES), shift_o), jnp.full((8, LANES), end_o)
            else:
                shift, end = jnp.where(lane >= begin, shift_o, shift), jnp.where(lane >= begin, end_o, end)
        index[t] = jnp.where(lane < end, (lane + shift) & (LANES - 1), -1)
        start = offs[o0] + jnp.minimum(base - o0 * CAP, counts[0, o0])
        place[t] = (start >> 7) + (lane < (start & (LANES - 1))).astype(jnp.int32)

    loads[1].wait()
    loads[2].wait()

    def snap(i, lanes):
        return x[0:3, i, lanes], x[3:6, i, lanes]

    def pair(ref, i, lanes):
        return ref[6 * i : 6 * i + 3, lanes], ref[6 * i + 3 : 6 * i + 6, lanes]

    def put(ref, i, lanes, value):
        ref[6 * i : 6 * i + 3, lanes], ref[6 * i + 3 : 6 * i + 6, lanes] = value

    for c in range(ROWS // CHUNK):
        lanes = slice(c * CHUNK, (c + 1) * CHUNK)
        p = [snap(i, lanes) for i in range(8)]
        d1 = detail_of(p[0], p[1], p[2], 1.0)
        d3 = detail_of(p[2], p[3], p[4], 1.0)
        d5 = detail_of(p[4], p[5], p[6], 1.0)
        e2 = updated(p[2], d1, d3)
        e4 = updated(p[4], d3, d5)
        for i, v in enumerate((p[0], d1, e2, e4)):
            put(to_left, i, lanes, v)
        for i, v in enumerate((e4, d5, p[6], p[7])):
            put(to_right, i, lanes, v)
        for i, v in enumerate((d1, d3, d5)):
            put(s0, i, lanes, v)
        s0[18:20, lanes] = d5[1][1:3]
        s0[20:24, lanes] = jnp.zeros((4, CHUNK), jnp.float32)
        s2[6:7, lanes] = (ids[0:1, lanes] + 1).astype(jnp.float32)
        s2[7:8, lanes] = jnp.zeros((1, CHUNK), jnp.float32)

    def pack(phase):
        src, dst = rows_of[phase], xs[phase]
        strips = PHASES[phase][0] // 8
        for t in range(SLOT_TILES):
            slots = index[t]
            live = slots >= 0
            slots = slots & (LANES - 1)
            where = place[t]
            low = max(0, (ROWS - (SLOT_TILES - t) * LANES) // LANES)
            high = min(t, ROWS // LANES - 1)
            lanes = slice((t % X_TILES) * LANES, (t % X_TILES + 1) * LANES)
            for strip in range(strips):
                rows = slice(8 * strip, 8 * strip + 8)
                block = src[rows, low * LANES : (low + 1) * LANES]
                for i in range(low + 1, high + 1):
                    block = jnp.where(where == i, src[rows, i * LANES : (i + 1) * LANES], block)
                taken = jnp.take_along_axis(block, slots, axis=1, mode="promise_in_bounds")
                dst[t // X_TILES, rows, lanes] = jnp.where(live, taken, 0.0)

    def remote(src, dst, send, recv, peer):
        return pltpu.make_async_remote_copy(
            src_ref=src, dst_ref=dst, send_sem=send, recv_sem=recv, device_id=peer, device_id_type=MESH
        )

    halos = [
        remote(to_left, from_right, halo_s.at[0], halo_r.at[0], {"tm": left}),
        remote(to_right, from_left, halo_s.at[1], halo_r.at[1], {"tm": right}),
        remote(edge, edge_in, halo_s.at[2], halo_r.at[2], {"tm": right}),
    ]

    def lanes_of(xp):
        return pl.ds(pl.multiple_of(xp * WIDE, LANES), WIDE)

    def x_send(k, p):
        xp, peer = x_peer(k)
        src = xs[p].at[xp] if p else u0.at[:, lanes_of(xp)]
        dst = xr[p].at[mx] if p else w0.at[:, lanes_of(mx)]
        return remote(src, dst, x_s.at[p, xp], x_r.at[p, mx], peer)

    def x_arrival(k, p):
        xp, peer = x_peer(k)
        src = xs[p].at[xp] if p else u0.at[:, lanes_of(xp)]
        dst = xr[p].at[xp] if p else w0.at[:, lanes_of(xp)]
        return remote(src, dst, x_s.at[p, xp], x_r.at[p, xp], peer)

    def z_send(k, p):
        z, peer = z_peer(k)
        return remote(zs[p].at[z], zr[p].at[mz], z_s.at[p, z], z_r.at[p, mz], peer)

    def z_arrival(k, p):
        z, peer = z_peer(k)
        return remote(zs[p].at[z], zr[p].at[z], z_s.at[p, z], z_r.at[p, z], peer)

    def x_out(p):
        for k in X_ORDER:
            x_send(k, p).start()
        if p:
            xr[p][mx] = xs[p][mx]
        else:
            w0[:, lanes_of(mx)] = u0[:, lanes_of(mx)]

    def x_in(p):
        for k in X_ORDER:
            x_arrival(k, p).wait_recv()

    def z_out(p, order):
        for k in order:
            z_send(k, p).start()

    def z_in(p):
        for k in FAR_FIRST:
            z_arrival(k, p).wait_recv()

    def piece(src, xp, strip, z, lane_to):
        rows = slice(8 * strip, 8 * strip + 8)
        begin = z * CAP
        t = begin // LANES
        block = src[xp, rows, t * LANES : (t + 1) * LANES]
        if begin + CAP > (t + 1) * LANES:
            after = src[xp, rows, (t + 1) * LANES : (t + 2) * LANES]
            block = jnp.where(lane >= begin - t * LANES, block, after)
        turn = (lane_to - begin) % LANES
        return pltpu.roll(block, turn, 1) if turn else block

    def joined(src, strip, z):
        out = piece(src, 0, strip, z, 0)
        for xp in range(1, NX):
            out = jnp.where(lane >= xp * CAP, piece(src, xp, strip, z, xp * CAP), out)
        return out

    pl.semaphore_wait(barrier, len(peers))
    halos[0].start()
    halos[1].start()
    for k in NEAR:
        pl.semaphore_signal(far_sem.at[(NZ - k) % NZ], inc=1, device_id=z_peer(k)[1], device_id_type=MESH)

    pack(0)
    for z in range(NZ):
        for i in range(2):
            last = jnp.where(row < 2, piece(xs0, i, 2, z, SPAN), piece(xs0, i + 2, 2, z, SPAN))
            zs0[z, 8 * i : 8 * i + 8, :] = jnp.where(spare, last, joined(xs0, i, z))
    z_out(0, NEAR)
    zr0[mz] = zs0[mz]

    halos[0].wait_recv()
    halos[1].wait_recv()

    for c in range(ROWS // CHUNK):
        lanes = slice(c * CHUNK, (c + 1) * CHUNK)
        x0, d1, e2, e4 = (pair(to_left, i, lanes) for i in range(4))
        d5, x6, x7 = (pair(to_right, i, lanes) for i in range(1, 4))
        x8, d9, e10, e12 = (pair(from_right, i, lanes) for i in range(4))
        em4, dm3, xm2, xm1 = (pair(from_left, i, lanes) for i in range(4))
        dm1 = detail_of(xm2, xm1, x0, 1.0)
        e0 = updated(x0, chosen(first, d1, dm1), d1)
        d7 = detail_of(x6, x7, x8, 1.0, final)
        e6 = updated(x6, d5, d7)
        e8 = updated(x8, d7, d9)
        em2 = updated(xm2, dm3, dm1)
        dm2 = detail_of(em4, em2, e0, 2.0)
        d2 = detail_of(e0, e2, e4, 2.0)
        d6 = detail_of(e4, e6, e8, 2.0, final)
        d10 = detail_of(e8, e10, e12, 2.0)
        f0 = updated(e0, chosen(first, d2, dm2), d2)
        f4 = updated(e4, d2, d6)
        f8 = updated(e8, d6, d10)
        d4 = detail_of(f0, f4, f8, 4.0, final)
        for i, v in enumerate((d2, d7, d6, d4)):
            put(s1, i, lanes, v)
        put(s2, 0, lanes, f0)
        put(edge, 0, lanes, d4)

    halos[2].start()
    pack(1)
    x_out(1)

    for k in FAR:
        if k <= NZ // 2:
            pl.semaphore_wait(far_sem.at[k - REACH], 1)
        if k >= NZ // 2:
            pl.semaphore_wait(far_sem.at[k + REACH], 1)
        z_send(k, 0).start()

    halos[2].wait_recv()
    d4 = edge[...]
    before = jnp.where(first, d4, edge_in[...])
    s2[0:6, :] = s2[0:6, :] + 0.25 * (before + d4)
    pack(2)
    x_out(2)

    x_in(1)
    for z in range(NZ):
        last = joined(xr1, 2, z)
        for i in range(2):
            zs1[z, 8 * i : 8 * i + 8, :] = jnp.where(spare, pltpu.roll(last, SPAN - 32 * i, 1), joined(xr1, i, z))
        zs2[z] = pltpu.roll(last, SPAN - 64, 1)
    z_out(1, FAR_FIRST)
    zr1[mz] = zs1[mz]

    x_in(2)
    for z in range(NZ):
        zs2[z] = jnp.where(spare, zs2[z], joined(xr2, 0, z))
    z_out(2, FAR_FIRST)
    zr2[mz] = zs2[mz]

    def unpack(u, strip, part):
        rows = slice(8 * strip, 8 * strip + 8)
        for xp in range(NX):
            tiles = [None] * X_TILES
            for z in range(NZ):
                block, begin = part(z, xp)
                turn = (z * CAP - begin) % LANES
                turned = pltpu.roll(block, turn, 1) if turn else block
                for t in range(X_TILES):
                    low, high = z * CAP - t * LANES, (z + 1) * CAP - t * LANES
                    if high > 0 and low < LANES:
                        old = tiles[t]
                        tiles[t] = turned if old is None else jnp.where(lane >= low, turned, old)
            for t in range(X_TILES):
                at = (xp * X_TILES + t) * LANES
                u[rows, at : at + LANES] = tiles[t]

    z_in(0)
    for strip in range(2):
        unpack(u0, strip, lambda z, xp: (zr0[z, 8 * strip : 8 * strip + 8, :], xp * CAP))
    unpack(u0, 2, lambda z, xp: (zr0[z, 8 * (xp % 2) : 8 * (xp % 2) + 8, :], SPAN))
    half = NX * WIDE // 2
    u0[16:18, half:] = u0[18:20, half:]
    x_out(0)

    z_in(1)
    for strip in range(2):
        unpack(u1, strip, lambda z, xp: (zr1[z, 8 * strip : 8 * strip + 8, :], xp * CAP))
    coef[2] = u1[0:6, :]
    coef[7] = u1[6:12, :]
    coef[6, 0:4] = u1[12:16, :]
    for z in range(NZ):
        low = pltpu.roll(zr1[z, 0:8, :], 32, 1)
        tail[z] = jnp.where(lane < 32, low, pltpu.roll(zr1[z, 8:16, :], 64, 1))

    z_in(2)
    unpack(u1, 3, lambda z, xp: (zr2[z], xp * CAP))
    coef[0] = u1[24:30, :]
    x_in(0)
    coef[1] = w0[0:6, :]
    coef[3] = w0[6:12, :]
    coef[5] = w0[12:18, :]
    for t in range(SLOT_TILES):
        oid[t : t + 1, :] = u1[30:31, t * LANES : (t + 1) * LANES].astype(jnp.int32) - 1
    for z in range(NZ):
        tail[z] = jnp.where(lane < 64, tail[z], pltpu.roll(zr2[z], 96, 1))
    unpack(u1, 2, lambda z, xp: (tail[z], xp * CAP))
    coef[6, 4:6] = u1[16:18, :]
    coef[4] = u1[18:24, :]

    for halo in halos:
        halo.wait_send()
    for p in range(3):
        for k in X_ORDER:
            x_send(k, p).wait_send()
        for k in FAR_FIRST:
            z_send(k, p).wait_send()


def per_device(trajectory, counts, particle_ids):
    f32, i32 = jnp.float32, jnp.int32
    vmem = lambda *shape: pltpu.VMEM(shape, f32)
    dma = pltpu.SemaphoreType.DMA
    slots = NX * WIDE
    coefficients, owned = pl.pallas_call(
        kernel,
        out_shape=(pltpu.VMEM((8, 6, slots), f32), pltpu.VMEM((SLOT_TILES, LANES), i32)),
        in_specs=[pl.BlockSpec(memory_space=pltpu.HBM)] * 3,
        out_specs=(pl.BlockSpec(memory_space=pltpu.VMEM), pl.BlockSpec(memory_space=pltpu.VMEM)),
        scratch_shapes=[
            pltpu.SMEM((1, NX * NZ), i32), pltpu.VMEM((1, ROWS), i32), vmem(6, 8, ROWS),
            *[vmem(rows, ROWS) for rows, _ in PHASES],
            vmem(24, ROWS), vmem(24, ROWS), vmem(24, ROWS), vmem(24, ROWS),
            vmem(6, ROWS), vmem(6, ROWS),
            pltpu.VMEM((SLOT_TILES, 8, LANES), i32), pltpu.VMEM((SLOT_TILES, 8, LANES), i32),
            pltpu.SMEM((NX * NZ,), i32),
            *[vmem(NX, rows, WIDE) for rows, _ in PHASES],
            *[vmem(NX, rows, WIDE) for rows, _ in PHASES],
            *[vmem(NZ, 8 * tiles, LANES) for _, tiles in PHASES],
            *[vmem(NZ, 8 * tiles, LANES) for _, tiles in PHASES],
            vmem(NZ, 8, LANES), vmem(24, slots), vmem(32, slots), vmem(24, slots),
            dma((3,)), pltpu.SemaphoreType.REGULAR((NZ,)), dma((3,)), dma((3,)),
            dma((3, NZ)), dma((3, NZ)), dma((3, NX)), dma((3, NX)),
        ],
        compiler_params=pltpu.CompilerParams(
            collective_id=0, has_side_effects=True, vmem_limit_bytes=60 * 2**20
        ),
        name="regroup_and_lift",
    )(counts, particle_ids.reshape(1, ROWS), trajectory.transpose(1, 0, 2))
    return coefficients, owned.reshape(slots)


def solution(mesh):
    return jax.shard_map(
        per_device,
        mesh=mesh,
        in_specs=(P("tm", None, "space"), P("space", None), P("space")),
        out_specs=(P("tm", None, "space"), P("space")),
        check_vma=False,
    )
```

```python
import functools

import jax
import jax.numpy as jnp
from jax import lax
from jax.experimental import pallas as pl
from jax.experimental.pallas import tpu as pltpu
from jax.sharding import PartitionSpec as P

MESH = pl.DeviceIdType.MESH
NX = 4
NZ = 16
NT = 8
CAP = 24
ROWS = 1024
LANES = 128
SLOT_TILES = NX * NZ * CAP // LANES
WIDE = NZ * CAP
X_TILES = WIDE // LANES
CHUNK = 256
X_ORDER = (2, 1, 3)
REACH = 4
NEAR = (4, 12, 3, 13, 2, 14, 1, 15)
FAR = (5, 11, 6, 10, 7, 9, 8)
FAR_FIRST = (8, 7, 9, 6, 10, 5, 11) + NEAR
SPAN = NX * CAP
PHASES = ((24, 2), (16, 1), (16, 1), (16, 1))
Z_FIRST = (0, 1)


def wrapped(delta):
    return delta - 4.0 * jnp.floor(delta * 0.25 + 0.5)


def detail_of(start, odd, finish, h, final=None):
    (xa, va), (xo, vo), (xb, vb) = start, odd, finish
    shift = wrapped(xb - xa)
    guess_x = xa + 0.5 * shift + (0.25 * h) * (va - vb)
    guess_v = (0.75 / h) * shift - 0.25 * (va + vb)
    if final is not None:
        guess_x = jnp.where(final, xa + h * va, guess_x)
        guess_v = jnp.where(final, va, guess_v)
    return wrapped(xo - guess_x), vo - guess_v


def updated(even, left, right):
    return tuple(e + 0.25 * (a + b) for e, a, b in zip(even, left, right))


def chosen(flag, a, b):
    return tuple(jnp.where(flag, p, q) for p, q in zip(a, b))


def kernel(
    counts_hbm, ids_hbm, traj, coef, oid,
    counts, ids, x, to_left, to_right, from_right, from_left, edge, edge_in, even, index, place, offs, *refs
):
    rows_of, xs, xr, zs, zr, u, w = (refs[4 * i : 4 * i + 4] for i in range(7))
    load_sem, far_sem, halo_s, halo_r, z_s, z_r, x_s, x_r = refs[28:]
    me = lax.axis_index("space")
    mx, mz = me // NZ, me % NZ
    mt = lax.axis_index("tm")
    first, final = mt == 0, mt == NT - 1
    left, right = (mt + NT - 1) % NT, (mt + 1) % NT

    def z_peer(k):
        z = (mz + k) % NZ
        return z, {"space": mx * NZ + z}

    def x_peer(k):
        xp = (mx + k) % NX
        return xp, {"space": xp * NZ + mz}

    barrier = pltpu.get_barrier_semaphore()
    peers = [z_peer(k)[1] for k in NEAR] + [x_peer(k)[1] for k in X_ORDER]
    peers += [{"tm": left}, {"tm": right}]
    for peer in peers:
        pl.semaphore_signal(barrier, inc=1, device_id=peer, device_id_type=MESH)

    loads = [
        pltpu.make_async_copy(counts_hbm, counts, load_sem.at[0]),
        pltpu.make_async_copy(traj, x, load_sem.at[1]),
        pltpu.make_async_copy(ids_hbm, ids, load_sem.at[2]),
    ]
    for load in loads:
        load.start()
    loads[0].wait()
    total = jnp.int32(0)
    for o in range(NX * NZ):
        offs[o] = total
        total = total + counts[0, o]

    lane = lax.broadcasted_iota(jnp.int32, (8, LANES), 1)
    row = lax.broadcasted_iota(jnp.int32, (8, LANES), 0)
    spare = lane >= SPAN

    for t in range(SLOT_TILES):
        base = t * LANES
        o0 = base // CAP
        shift, end = None, None
        for o in range(o0, (base + LANES - 1) // CAP + 1):
            begin = o * CAP - base
            shift_o, end_o = offs[o] - begin, begin + counts[0, o]
            if shift is None:
                shift, end = jnp.full((8, LANES), shift_o), jnp.full((8, LANES), end_o)
            else:
                shift, end = jnp.where(lane >= begin, shift_o, shift), jnp.where(lane >= begin, end_o, end)
        index[t] = jnp.where(lane < end, (lane + shift) & (LANES - 1), -1)
        start = offs[o0] + jnp.minimum(base - o0 * CAP, counts[0, o0])
        place[t] = (start >> 7) + (lane < (start & (LANES - 1))).astype(jnp.int32)

    loads[1].wait()
    loads[2].wait()

    def snap(i, lanes):
        return x[0:3, i, lanes], x[3:6, i, lanes]

    def pair(ref, i, lanes):
        return ref[6 * i : 6 * i + 3, lanes], ref[6 * i + 3 : 6 * i + 6, lanes]

    def put(ref, i, lanes, value):
        ref[6 * i : 6 * i + 3, lanes], ref[6 * i + 3 : 6 * i + 6, lanes] = value

    for c in range(ROWS // CHUNK):
        lanes = slice(c * CHUNK, (c + 1) * CHUNK)
        p = [snap(i, lanes) for i in range(8)]
        d1 = detail_of(p[0], p[1], p[2], 1.0)
        d3 = detail_of(p[2], p[3], p[4], 1.0)
        d5 = detail_of(p[4], p[5], p[6], 1.0)
        e2 = updated(p[2], d1, d3)
        e4 = updated(p[4], d3, d5)
        for i, v in enumerate((p[0], d1, e2, e4)):
            put(to_left, i, lanes, v)
        for i, v in enumerate((e4, d5, p[6], p[7])):
            put(to_right, i, lanes, v)
        for i, v in enumerate((d1, d3, d5)):
            put(rows_of[0], i, lanes, v)
        tag = (ids[0:1, lanes] + 1).astype(jnp.float32)
        rows_of[0][18:19, lanes] = tag
        rows_of[0][20:22, lanes] = d5[1][1:3]
        rows_of[0][22:23, lanes] = tag

    def spread(r, lanes, value):
        n = value.shape[0]
        i = 0
        while i < n:
            dst, at = rows_of[1 + (r + i) // 10], (r + i) % 10
            m = min(n - i, (8 if at < 8 else 10) - at)
            for again in range(1 if at < 8 else NX):
                dst[at + 2 * again : at + 2 * again + m, lanes] = value[i : i + m]
            i += m

    def pack(phase):
        src, dst = rows_of[phase], xs[phase]
        strips = PHASES[phase][0] // 8
        for t in range(SLOT_TILES):
            slots = index[t]
            live = slots >= 0
            slots = slots & (LANES - 1)
            where = place[t]
            low = max(0, (ROWS - (SLOT_TILES - t) * LANES) // LANES)
            high = min(t, ROWS // LANES - 1)
            lanes = slice((t % X_TILES) * LANES, (t % X_TILES + 1) * LANES)
            for strip in range(strips):
                rows = slice(8 * strip, 8 * strip + 8)
                block = src[rows, low * LANES : (low + 1) * LANES]
                for i in range(low + 1, high + 1):
                    block = jnp.where(where == i, src[rows, i * LANES : (i + 1) * LANES], block)
                taken = jnp.take_along_axis(block, slots, axis=1, mode="promise_in_bounds")
                dst[t // X_TILES, rows, lanes] = jnp.where(live, taken, 0.0)

    def remote(src, dst, send, recv, peer):
        return pltpu.make_async_remote_copy(
            src_ref=src, dst_ref=dst, send_sem=send, recv_sem=recv, device_id=peer, device_id_type=MESH
        )

    halos = [
        remote(to_left, from_right, halo_s.at[0], halo_r.at[0], {"tm": left}),
        remote(to_right, from_left, halo_s.at[1], halo_r.at[1], {"tm": right}),
        remote(edge, edge_in, halo_s.at[2], halo_r.at[2], {"tm": right}),
    ]

    def lanes_of(xp):
        return pl.ds(pl.multiple_of(xp * WIDE, LANES), WIDE)

    def x_refs(p, there, here):
        if p in Z_FIRST:
            return u[p].at[:, lanes_of(there)], w[p].at[:, lanes_of(here)]
        return xs[p].at[there], xr[p].at[here]

    def x_send(k, p):
        xp, peer = x_peer(k)
        src, dst = x_refs(p, xp, mx)
        return remote(src, dst, x_s.at[p, xp], x_r.at[p, mx], peer)

    def x_arrival(k, p):
        xp, peer = x_peer(k)
        src, dst = x_refs(p, xp, xp)
        return remote(src, dst, x_s.at[p, xp], x_r.at[p, xp], peer)

    def z_send(k, p):
        z, peer = z_peer(k)
        return remote(zs[p].at[z], zr[p].at[mz], z_s.at[p, z], z_r.at[p, mz], peer)

    def z_arrival(k, p):
        z, peer = z_peer(k)
        return remote(zs[p].at[z], zr[p].at[z], z_s.at[p, z], z_r.at[p, z], peer)

    def x_out(p):
        for k in X_ORDER:
            x_send(k, p).start()
        if p in Z_FIRST:
            w[p][:, lanes_of(mx)] = u[p][:, lanes_of(mx)]
        else:
            xr[p][mx] = xs[p][mx]

    def x_in(p):
        for k in X_ORDER:
            x_arrival(k, p).wait_recv()

    def z_out(p, order):
        for k in order:
            if p == 0 and k in FAR:
                if k <= NZ // 2:
                    pl.semaphore_wait(far_sem.at[k - REACH], 1)
                if k >= NZ // 2:
                    pl.semaphore_wait(far_sem.at[k + REACH], 1)
            z_send(k, p).start()

    def z_in(p):
        for k in FAR_FIRST:
            z_arrival(k, p).wait_recv()

    def blocks_of(src, strip):
        rows = slice(8 * strip, 8 * strip + 8)
        return [
            [src[xp, rows, t * LANES : (t + 1) * LANES] for t in range(X_TILES)] for xp in range(NX)
        ]

    def piece(blocks, xp, z, lane_to):
        begin = z * CAP
        t = begin // LANES
        block = blocks[xp][t]
        if begin + CAP > (t + 1) * LANES:
            block = jnp.where(lane >= begin - t * LANES, block, blocks[xp][t + 1])
        turn = (lane_to - begin) % LANES
        return pltpu.roll(block, turn, 1) if turn else block

    def joined(blocks, z):
        out = piece(blocks, 0, z, 0)
        for xp in range(1, NX):
            out = jnp.where(lane >= xp * CAP, piece(blocks, xp, z, xp * CAP), out)
        return out

    pl.semaphore_wait(barrier, len(peers))
    halos[0].start()
    halos[1].start()
    for k in NEAR:
        pl.semaphore_signal(far_sem.at[(NZ - k) % NZ], inc=1, device_id=z_peer(k)[1], device_id_type=MESH)

    def join(p, src):
        tiles = PHASES[p][1]
        per = NX // tiles
        last = blocks_of(src, tiles)
        for i in range(tiles):
            blocks = blocks_of(src, i)
            for z in range(NZ):
                more = piece(last, i, z, SPAN)
                for j in range(1, per):
                    more = jnp.where(row < 8 // per * j, more, piece(last, i + tiles * j, z, SPAN))
                zs[p][z, 8 * i : 8 * i + 8, :] = jnp.where(spare, more, joined(blocks, z))

    def own_z(p):
        zr[p][mz] = zs[p][mz]

    pack(0)
    join(0, xs[0])
    z_out(0, NEAR)
    z_out(0, FAR[:4])

    halos[0].wait_recv()
    halos[1].wait_recv()

    for c in range(ROWS // CHUNK):
        lanes = slice(c * CHUNK, (c + 1) * CHUNK)
        x0, d1, e2, e4 = (pair(to_left, i, lanes) for i in range(4))
        d5, x6, x7 = (pair(to_right, i, lanes) for i in range(1, 4))
        x8, d9, e10, e12 = (pair(from_right, i, lanes) for i in range(4))
        em4, dm3, xm2, xm1 = (pair(from_left, i, lanes) for i in range(4))
        dm1 = detail_of(xm2, xm1, x0, 1.0)
        e0 = updated(x0, chosen(first, d1, dm1), d1)
        d7 = detail_of(x6, x7, x8, 1.0, final)
        e6 = updated(x6, d5, d7)
        e8 = updated(x8, d7, d9)
        em2 = updated(xm2, dm3, dm1)
        dm2 = detail_of(em4, em2, e0, 2.0)
        d2 = detail_of(e0, e2, e4, 2.0)
        d6 = detail_of(e4, e6, e8, 2.0, final)
        d10 = detail_of(e8, e10, e12, 2.0)
        f0 = updated(e0, chosen(first, d2, dm2), d2)
        f4 = updated(e4, d2, d6)
        f8 = updated(e8, d6, d10)
        d4 = detail_of(f0, f4, f8, 4.0, final)
        for i, v in enumerate((d7, d6, d2, d4)):
            spread(6 * i, lanes, v[0])
            spread(6 * i + 3, lanes, v[1])
        put(even, 0, lanes, f0)
        put(edge, 0, lanes, d4)

    halos[2].start()
    pack(2)
    x_out(2)
    z_out(0, FAR[4:])
    pack(1)
    join(1, xs[1])
    z_out(1, FAR_FIRST)
    own_z(0)
    own_z(1)

    halos[2].wait_recv()
    d4 = edge[...]
    before = jnp.where(first, d4, edge_in[...])
    spread(24, slice(None), even[...] + 0.25 * (before + d4))
    pack(3)
    x_out(3)

    x_in(2)
    join(2, xr[2])
    z_out(2, FAR_FIRST)
    own_z(2)
    x_in(3)
    join(3, xr[3])
    z_out(3, FAR_FIRST)
    own_z(3)

    def unpack(dst, at, n, part):
        for xp in range(NX):
            tiles = [None] * X_TILES
            for z in range(NZ):
                block, begin, skip = part(z, xp)
                turn = (z * CAP - begin) % LANES
                turned = pltpu.roll(block, turn, 1) if turn else block
                for t in range(X_TILES):
                    low, high = z * CAP - t * LANES, (z + 1) * CAP - t * LANES
                    if high > 0 and low < LANES:
                        old = tiles[t]
                        tiles[t] = turned if old is None else jnp.where(lane >= low, turned, old)
            for t in range(X_TILES):
                lanes = slice((xp * X_TILES + t) * LANES, (xp * X_TILES + t + 1) * LANES)
                dst[at : at + n, lanes] = tiles[t][skip : skip + n]

    def unjoin(p, few):
        tiles = PHASES[p][1]
        per = NX // tiles
        for i in range(tiles):
            unpack(u[p], 8 * i, 8, lambda z, xp: (zr[p][z, 8 * i : 8 * i + 8, :], xp * CAP, 0))

        def rest(z, xp):
            i = xp % tiles
            return zr[p][z, 8 * i : 8 * i + 8, :], SPAN, 8 // per * (xp // tiles)

        unpack(u[p], 8 * tiles, few, rest)

    z_in(0)
    unjoin(0, 3)
    x_out(0)
    z_in(1)
    unjoin(1, 2)
    x_out(1)

    z_in(2)
    unjoin(2, 2)
    coef[6, 4:6] = u[2][0:2, :]
    coef[2] = u[2][2:8, :]
    coef[4, 0:2] = u[2][8:10, :]
    x_in(0)
    coef[1] = w[0][0:6, :]
    coef[3] = w[0][6:12, :]
    coef[5] = w[0][12:18, :]
    for t in range(SLOT_TILES):
        oid[t : t + 1, :] = w[0][18:19, t * LANES : (t + 1) * LANES].astype(jnp.int32) - 1
    x_in(1)
    coef[7] = w[1][0:6, :]
    coef[6, 0:4] = w[1][6:10, :]

    z_in(3)
    unjoin(3, 2)
    coef[4, 2:6] = u[3][0:4, :]
    coef[0] = u[3][4:10, :]

    for halo in halos:
        halo.wait_send()
    for p in range(len(PHASES)):
        for k in X_ORDER:
            x_send(k, p).wait_send()
        for k in FAR_FIRST:
            z_send(k, p).wait_send()


def per_device(trajectory, counts, particle_ids):
    f32, i32 = jnp.float32, jnp.int32
    vmem = lambda *shape: pltpu.VMEM(shape, f32)
    dma = pltpu.SemaphoreType.DMA
    slots = NX * WIDE
    coefficients, owned = pl.pallas_call(
        kernel,
        out_shape=(pltpu.VMEM((8, 6, slots), f32), pltpu.VMEM((SLOT_TILES, LANES), i32)),
        in_specs=[pl.BlockSpec(memory_space=pltpu.HBM)] * 3,
        out_specs=(pl.BlockSpec(memory_space=pltpu.VMEM), pl.BlockSpec(memory_space=pltpu.VMEM)),
        scratch_shapes=[
            pltpu.SMEM((1, NX * NZ), i32), pltpu.VMEM((1, ROWS), i32), vmem(6, 8, ROWS),
            vmem(24, ROWS), vmem(24, ROWS), vmem(24, ROWS), vmem(24, ROWS),
            vmem(6, ROWS), vmem(6, ROWS), vmem(6, ROWS),
            pltpu.VMEM((SLOT_TILES, 8, LANES), i32), pltpu.VMEM((SLOT_TILES, 8, LANES), i32),
            pltpu.SMEM((NX * NZ,), i32),
            *[vmem(rows, ROWS) for rows, _ in PHASES],
            *[vmem(NX, rows, WIDE) for rows, _ in PHASES],
            *[vmem(NX, rows, WIDE) for rows, _ in PHASES],
            *[vmem(NZ, 8 * tiles, LANES) for _, tiles in PHASES],
            *[vmem(NZ, 8 * tiles, LANES) for _, tiles in PHASES],
            *[vmem(rows, slots) for rows, _ in PHASES],
            *[vmem(rows, slots) for rows, _ in PHASES],
            dma((3,)), pltpu.SemaphoreType.REGULAR((NZ,)), dma((3,)), dma((3,)),
            dma((4, NZ)), dma((4, NZ)), dma((4, NX)), dma((4, NX)),
        ],
        compiler_params=pltpu.CompilerParams(
            collective_id=0, has_side_effects=True, vmem_limit_bytes=60 * 2**20
        ),
        name="regroup_and_lift",
    )(counts, particle_ids.reshape(1, ROWS), trajectory.transpose(1, 0, 2))
    return coefficients, owned.reshape(slots)


def solution(mesh):
    return jax.shard_map(
        per_device,
        mesh=mesh,
        in_specs=(P("tm", None, "space"), P("space", None), P("space")),
        out_specs=(P("tm", None, "space"), P("space")),
        check_vma=False,
    )
```

```python
import functools

import jax
import jax.numpy as jnp
from jax import lax
from jax.experimental import pallas as pl
from jax.experimental.pallas import tpu as pltpu
from jax.sharding import PartitionSpec as P

MESH = pl.DeviceIdType.MESH
NX = 4
NZ = 16
NT = 8
CAP = 24
ROWS = 1024
LANES = 128
SLOT_TILES = NX * NZ * CAP // LANES
WIDE = NZ * CAP
X_TILES = WIDE // LANES
CHUNK = 256
X_ORDER = (2, 1, 3)
REACH = 4
NEAR = (4, 12, 3, 13, 2, 14, 1, 15)
FAR = (5, 11, 6, 10, 7, 9, 8)
FAR_FIRST = (8, 7, 9, 6, 10, 5, 11) + NEAR
SPAN = NX * CAP
PHASES = ((24, 2), (16, 1), (16, 1), (16, 1))
Z_FIRST = (0, 1)


def wrapped(delta):
    return delta - 4.0 * jnp.floor(delta * 0.25 + 0.5)


def detail_of(start, odd, finish, h, final=None):
    (xa, va), (xo, vo), (xb, vb) = start, odd, finish
    shift = wrapped(xb - xa)
    guess_x = xa + 0.5 * shift + (0.25 * h) * (va - vb)
    guess_v = (0.75 / h) * shift - 0.25 * (va + vb)
    if final is not None:
        guess_x = jnp.where(final, xa + h * va, guess_x)
        guess_v = jnp.where(final, va, guess_v)
    return wrapped(xo - guess_x), vo - guess_v


def updated(even, left, right):
    return tuple(e + 0.25 * (a + b) for e, a, b in zip(even, left, right))


def chosen(flag, a, b):
    return tuple(jnp.where(flag, p, q) for p, q in zip(a, b))


def kernel(
    counts_hbm, ids_hbm, traj, coef, oid,
    counts, ids, x, to_left, to_right, from_right, from_left, edge, edge_in, even, index, place, offs, *refs
):
    rows_of, xs, xr, zs, zr, u, w = (refs[4 * i : 4 * i + 4] for i in range(7))
    load_sem, far_sem, halo_s, halo_r, z_s, z_r, x_s, x_r = refs[28:]
    me = lax.axis_index("space")
    mx, mz = me // NZ, me % NZ
    mt = lax.axis_index("tm")
    first, final = mt == 0, mt == NT - 1
    left, right = (mt + NT - 1) % NT, (mt + 1) % NT

    def z_peer(k):
        z = (mz + k) % NZ
        return z, {"space": mx * NZ + z}

    def x_peer(k):
        xp = (mx + k) % NX
        return xp, {"space": xp * NZ + mz}

    barrier = pltpu.get_barrier_semaphore()
    peers = [z_peer(k)[1] for k in NEAR] + [x_peer(k)[1] for k in X_ORDER]
    peers += [{"tm": left}, {"tm": right}]
    for peer in peers:
        pl.semaphore_signal(barrier, inc=1, device_id=peer, device_id_type=MESH)

    loads = [
        pltpu.make_async_copy(counts_hbm, counts, load_sem.at[0]),
        pltpu.make_async_copy(traj, x, load_sem.at[1]),
        pltpu.make_async_copy(ids_hbm, ids, load_sem.at[2]),
    ]
    for load in loads:
        load.start()
    loads[0].wait()
    total = jnp.int32(0)
    for o in range(NX * NZ):
        offs[o] = total
        total = total + counts[0, o]

    lane = lax.broadcasted_iota(jnp.int32, (8, LANES), 1)
    row = lax.broadcasted_iota(jnp.int32, (8, LANES), 0)
    spare = lane >= SPAN

    for t in range(SLOT_TILES):
        base = t * LANES
        o0 = base // CAP
        shift, end = None, None
        for o in range(o0, (base + LANES - 1) // CAP + 1):
            begin = o * CAP - base
            shift_o, end_o = offs[o] - begin, begin + counts[0, o]
            if shift is None:
                shift, end = jnp.full((8, LANES), shift_o), jnp.full((8, LANES), end_o)
            else:
                shift, end = jnp.where(lane >= begin, shift_o, shift), jnp.where(lane >= begin, end_o, end)
        index[t] = jnp.where(lane < end, (lane + shift) & (LANES - 1), -1)
        start = offs[o0] + jnp.minimum(base - o0 * CAP, counts[0, o0])
        place[t] = (start >> 7) + (lane < (start & (LANES - 1))).astype(jnp.int32)

    loads[1].wait()
    loads[2].wait()

    def snap(i, lanes):
        return x[0:3, i, lanes], x[3:6, i, lanes]

    def pair(ref, i, lanes):
        return ref[6 * i : 6 * i + 3, lanes], ref[6 * i + 3 : 6 * i + 6, lanes]

    def put(ref, i, lanes, value):
        ref[6 * i : 6 * i + 3, lanes], ref[6 * i + 3 : 6 * i + 6, lanes] = value

    for c in range(ROWS // CHUNK):
        lanes = slice(c * CHUNK, (c + 1) * CHUNK)
        p = [snap(i, lanes) for i in range(8)]
        d1 = detail_of(p[0], p[1], p[2], 1.0)
        d3 = detail_of(p[2], p[3], p[4], 1.0)
        d5 = detail_of(p[4], p[5], p[6], 1.0)
        e2 = updated(p[2], d1, d3)
        e4 = updated(p[4], d3, d5)
        for i, v in enumerate((p[0], d1, e2, e4)):
            put(to_left, i, lanes, v)
        for i, v in enumerate((e4, d5, p[6], p[7])):
            put(to_right, i, lanes, v)
        for i, v in enumerate((d1, d3, d5)):
            put(rows_of[0], i, lanes, v)
        tag = (ids[0:1, lanes] + 1).astype(jnp.float32)
        rows_of[0][18:19, lanes] = tag
        rows_of[0][20:22, lanes] = d5[1][1:3]
        rows_of[0][22:23, lanes] = tag

    def spread(r, lanes, value):
        n = value.shape[0]
        i = 0
        while i < n:
            dst, at = rows_of[1 + (r + i) // 10], (r + i) % 10
            m = min(n - i, (8 if at < 8 else 10) - at)
            for again in range(1 if at < 8 else NX):
                dst[at + 2 * again : at + 2 * again + m, lanes] = value[i : i + m]
            i += m

    def pack(phase):
        src, dst = rows_of[phase], xs[phase]
        strips = PHASES[phase][0] // 8
        for t in range(SLOT_TILES):
            slots = index[t]
            live = slots >= 0
            slots = slots & (LANES - 1)
            where = place[t]
            low = max(0, (ROWS - (SLOT_TILES - t) * LANES) // LANES)
            high = min(t, ROWS // LANES - 1)
            lanes = slice((t % X_TILES) * LANES, (t % X_TILES + 1) * LANES)
            for strip in range(strips):
                rows = slice(8 * strip, 8 * strip + 8)
                block = src[rows, low * LANES : (low + 1) * LANES]
                for i in range(low + 1, high + 1):
                    block = jnp.where(where == i, src[rows, i * LANES : (i + 1) * LANES], block)
                taken = jnp.take_along_axis(block, slots, axis=1, mode="promise_in_bounds")
                dst[t // X_TILES, rows, lanes] = jnp.where(live, taken, 0.0)

    def remote(src, dst, send, recv, peer):
        return pltpu.make_async_remote_copy(
            src_ref=src, dst_ref=dst, send_sem=send, recv_sem=recv, device_id=peer, device_id_type=MESH
        )

    halos = [
        remote(to_left, from_right, halo_s.at[0], halo_r.at[0], {"tm": left}),
        remote(to_right, from_left, halo_s.at[1], halo_r.at[1], {"tm": right}),
        remote(edge, edge_in, halo_s.at[2], halo_r.at[2], {"tm": right}),
    ]

    def lanes_of(xp):
        return pl.ds(pl.multiple_of(xp * WIDE, LANES), WIDE)

    def x_refs(p, there, here):
        if p in Z_FIRST:
            return u[p].at[:, lanes_of(there)], w[p].at[:, lanes_of(here)]
        return xs[p].at[there], xr[p].at[here]

    def x_send(k, p):
        xp, peer = x_peer(k)
        src, dst = x_refs(p, xp, mx)
        return remote(src, dst, x_s.at[p, xp], x_r.at[p, mx], peer)

    def x_arrival(k, p):
        xp, peer = x_peer(k)
        src, dst = x_refs(p, xp, xp)
        return remote(src, dst, x_s.at[p, xp], x_r.at[p, xp], peer)

    def z_send(k, p):
        z, peer = z_peer(k)
        return remote(zs[p].at[z], zr[p].at[mz], z_s.at[p, z], z_r.at[p, mz], peer)

    def z_arrival(k, p):
        z, peer = z_peer(k)
        return remote(zs[p].at[z], zr[p].at[z], z_s.at[p, z], z_r.at[p, z], peer)

    def x_out(p):
        for k in X_ORDER:
            x_send(k, p).start()
        if p in Z_FIRST:
            w[p][:, lanes_of(mx)] = u[p][:, lanes_of(mx)]
        else:
            xr[p][mx] = xs[p][mx]

    def x_in(p):
        for k in X_ORDER:
            x_arrival(k, p).wait_recv()

    def z_out(p, order):
        for k in order:
            if p == 0 and k in FAR:
                if k <= NZ // 2:
                    pl.semaphore_wait(far_sem.at[k - REACH], 1)
                if k >= NZ // 2:
                    pl.semaphore_wait(far_sem.at[k + REACH], 1)
            z_send(k, p).start()

    def z_part(p, low, high, order=FAR_FIRST):
        for k in order:
            z = (mz + k) % NZ
            pl.when((z >= low) & (z < high))(lambda k=k: z_send(k, p).start())

    def z_in(p):
        for k in FAR_FIRST:
            z_arrival(k, p).wait_recv()

    def blocks_of(src, strip):
        rows = slice(8 * strip, 8 * strip + 8)
        return [
            [src[xp, rows, t * LANES : (t + 1) * LANES] for t in range(X_TILES)] for xp in range(NX)
        ]

    def piece(blocks, xp, z, lane_to):
        begin = z * CAP
        t = begin // LANES
        block = blocks[xp][t]
        if begin + CAP > (t + 1) * LANES:
            block = jnp.where(lane >= begin - t * LANES, block, blocks[xp][t + 1])
        turn = (lane_to - begin) % LANES
        return pltpu.roll(block, turn, 1) if turn else block

    def joined(blocks, z):
        out = piece(blocks, 0, z, 0)
        for xp in range(1, NX):
            out = jnp.where(lane >= xp * CAP, piece(blocks, xp, z, xp * CAP), out)
        return out

    pl.semaphore_wait(barrier, len(peers))
    for k in NEAR:
        pl.semaphore_signal(far_sem.at[(NZ - k) % NZ], inc=1, device_id=z_peer(k)[1], device_id_type=MESH)

    halos[0].start()
    halos[1].start()

    def join(p, src):
        tiles = PHASES[p][1]
        per = NX // tiles
        last = blocks_of(src, tiles)
        for i in range(tiles):
            blocks = blocks_of(src, i)
            for z in range(NZ):
                more = piece(last, i, z, SPAN)
                for j in range(1, per):
                    more = jnp.where(row < 8 // per * j, more, piece(last, i + tiles * j, z, SPAN))
                zs[p][z, 8 * i : 8 * i + 8, :] = jnp.where(spare, more, joined(blocks, z))

    def own_z(p):
        zr[p][mz] = zs[p][mz]

    pack(0)
    join(0, xs[0])
    z_out(0, NEAR)
    z_out(0, FAR[:6])

    halos[0].wait_recv()
    halos[1].wait_recv()

    for c in range(ROWS // CHUNK):
        lanes = slice(c * CHUNK, (c + 1) * CHUNK)
        x0, d1, e2, e4 = (pair(to_left, i, lanes) for i in range(4))
        d5, x6, x7 = (pair(to_right, i, lanes) for i in range(1, 4))
        x8, d9, e10, e12 = (pair(from_right, i, lanes) for i in range(4))
        em4, dm3, xm2, xm1 = (pair(from_left, i, lanes) for i in range(4))
        dm1 = detail_of(xm2, xm1, x0, 1.0)
        e0 = updated(x0, chosen(first, d1, dm1), d1)
        d7 = detail_of(x6, x7, x8, 1.0, final)
        e6 = updated(x6, d5, d7)
        e8 = updated(x8, d7, d9)
        em2 = updated(xm2, dm3, dm1)
        dm2 = detail_of(em4, em2, e0, 2.0)
        d2 = detail_of(e0, e2, e4, 2.0)
        d6 = detail_of(e4, e6, e8, 2.0, final)
        d10 = detail_of(e8, e10, e12, 2.0)
        f0 = updated(e0, chosen(first, d2, dm2), d2)
        f4 = updated(e4, d2, d6)
        f8 = updated(e8, d6, d10)
        d4 = detail_of(f0, f4, f8, 4.0, final)
        for i, v in enumerate((d7, d6, d2, d4)):
            spread(6 * i, lanes, v[0])
            spread(6 * i + 3, lanes, v[1])
        put(even, 0, lanes, f0)
        put(edge, 0, lanes, d4)

    halos[2].start()
    pack(2)
    x_out(2)
    z_out(0, FAR[6:])
    pack(1)
    join(1, xs[1])
    z_part(1, 0, 4)
    z_part(1, 4, 16)
    own_z(0)
    own_z(1)

    halos[2].wait_recv()
    d4 = edge[...]
    before = jnp.where(first, d4, edge_in[...])
    spread(24, slice(None), even[...] + 0.25 * (before + d4))
    pack(3)
    x_out(3)

    x_in(2)
    join(2, xr[2])
    z_part(2, 0, 4)
    own_z(2)
    x_in(3)
    join(3, xr[3])
    z_part(3, 0, 2)
    z_part(3, 2, 4)
    z_part(2, 4, 16, FAR_FIRST[:7])
    z_part(3, 4, 16, FAR_FIRST[:7])
    z_part(2, 4, 16, NEAR)
    z_part(3, 4, 16, NEAR)
    own_z(3)

    def unpack(dst, at, n, part):
        for xp in range(NX):
            tiles = [None] * X_TILES
            for z in range(NZ):
                block, begin, skip = part(z, xp)
                turn = (z * CAP - begin) % LANES
                turned = pltpu.roll(block, turn, 1) if turn else block
                for t in range(X_TILES):
                    low, high = z * CAP - t * LANES, (z + 1) * CAP - t * LANES
                    if high > 0 and low < LANES:
                        old = tiles[t]
                        tiles[t] = turned if old is None else jnp.where(lane >= low, turned, old)
            for t in range(X_TILES):
                lanes = slice((xp * X_TILES + t) * LANES, (xp * X_TILES + t + 1) * LANES)
                dst[at : at + n, lanes] = tiles[t][skip : skip + n]

    def unjoin(p, few):
        tiles = PHASES[p][1]
        per = NX // tiles
        for i in range(tiles):
            unpack(u[p], 8 * i, 8, lambda z, xp: (zr[p][z, 8 * i : 8 * i + 8, :], xp * CAP, 0))

        def rest(z, xp):
            i = xp % tiles
            return zr[p][z, 8 * i : 8 * i + 8, :], SPAN, 8 // per * (xp // tiles)

        unpack(u[p], 8 * tiles, few, rest)

    z_in(0)
    unjoin(0, 3)
    x_out(0)
    z_in(1)
    unjoin(1, 2)
    x_out(1)

    z_in(2)
    unjoin(2, 2)
    coef[4:6, 6, :] = u[2][0:2, :]
    coef[0:6, 2, :] = u[2][2:8, :]
    coef[0:2, 4, :] = u[2][8:10, :]
    x_in(0)
    coef[0:6, 1, :] = w[0][0:6, :]
    coef[0:6, 3, :] = w[0][6:12, :]
    coef[0:6, 5, :] = w[0][12:18, :]
    for t in range(SLOT_TILES):
        oid[t : t + 1, :] = w[0][18:19, t * LANES : (t + 1) * LANES].astype(jnp.int32) - 1
    x_in(1)
    coef[0:6, 7, :] = w[1][0:6, :]
    coef[0:4, 6, :] = w[1][6:10, :]

    z_in(3)
    unjoin(3, 2)
    coef[2:6, 4, :] = u[3][0:4, :]
    coef[0:6, 0, :] = u[3][4:10, :]

    for halo in halos:
        halo.wait_send()
    for p in range(len(PHASES)):
        for k in X_ORDER:
            x_send(k, p).wait_send()
        for k in FAR_FIRST:
            z_send(k, p).wait_send()


def per_device(trajectory, counts, particle_ids):
    f32, i32 = jnp.float32, jnp.int32
    vmem = lambda *shape: pltpu.VMEM(shape, f32)
    dma = pltpu.SemaphoreType.DMA
    slots = NX * WIDE
    coefficients, owned = pl.pallas_call(
        kernel,
        out_shape=(pltpu.VMEM((6, 8, slots), f32), pltpu.VMEM((SLOT_TILES, LANES), i32)),
        in_specs=[pl.BlockSpec(memory_space=pltpu.HBM)] * 3,
        out_specs=(pl.BlockSpec(memory_space=pltpu.VMEM), pl.BlockSpec(memory_space=pltpu.VMEM)),
        scratch_shapes=[
            pltpu.SMEM((1, NX * NZ), i32), pltpu.VMEM((1, ROWS), i32), vmem(6, 8, ROWS),
            vmem(24, ROWS), vmem(24, ROWS), vmem(24, ROWS), vmem(24, ROWS),
            vmem(6, ROWS), vmem(6, ROWS), vmem(6, ROWS),
            pltpu.VMEM((SLOT_TILES, 8, LANES), i32), pltpu.VMEM((SLOT_TILES, 8, LANES), i32),
            pltpu.SMEM((NX * NZ,), i32),
            *[vmem(rows, ROWS) for rows, _ in PHASES],
            *[vmem(NX, rows, WIDE) for rows, _ in PHASES],
            *[vmem(NX, rows, WIDE) for rows, _ in PHASES],
            *[vmem(NZ, 8 * tiles, LANES) for _, tiles in PHASES],
            *[vmem(NZ, 8 * tiles, LANES) for _, tiles in PHASES],
            *[vmem(rows, slots) for rows, _ in PHASES],
            *[vmem(rows, slots) for rows, _ in PHASES],
            dma((3,)), pltpu.SemaphoreType.REGULAR((NZ,)), dma((3,)), dma((3,)),
            dma((4, NZ)), dma((4, NZ)), dma((4, NX)), dma((4, NX)),
        ],
        compiler_params=pltpu.CompilerParams(
            collective_id=0, has_side_effects=True, vmem_limit_bytes=60 * 2**20
        ),
        name="regroup_and_lift",
    )(counts, particle_ids.reshape(1, ROWS), trajectory.transpose(1, 0, 2))
    return coefficients.transpose(1, 0, 2), owned.reshape(slots)


def solution(mesh):
    return jax.shard_map(
        per_device,
        mesh=mesh,
        in_specs=(P("tm", None, "space"), P("space", None), P("space")),
        out_specs=(P("tm", None, "space"), P("space")),
        check_vma=False,
    )
```

```python
import functools

import jax
import jax.numpy as jnp
from jax import lax
from jax.experimental import pallas as pl
from jax.experimental.pallas import tpu as pltpu
from jax.sharding import PartitionSpec as P

MESH = pl.DeviceIdType.MESH
NX = 4
NZ = 16
NT = 8
CAP = 24
ROWS = 1024
LANES = 128
SLOT_TILES = NX * NZ * CAP // LANES
WIDE = NZ * CAP
X_TILES = WIDE // LANES
CHUNK = 256
X_ORDER = (2, 1, 3)
REACH = 4
NEAR = (4, 12, 3, 13, 2, 14, 1, 15)
FAR = (5, 11, 6, 10, 7, 9, 8)
FAR_FIRST = (8, 7, 9, 6, 10, 5, 11) + NEAR
SPAN = NX * CAP
PHASES = ((24, 2), (16, 1), (16, 1), (16, 1))
Z_FIRST = (0, 1)


def wrapped(delta):
    return delta - 4.0 * jnp.floor(delta * 0.25 + 0.5)


def detail_of(start, odd, finish, h, final=None):
    (xa, va), (xo, vo), (xb, vb) = start, odd, finish
    shift = wrapped(xb - xa)
    guess_x = xa + 0.5 * shift + (0.25 * h) * (va - vb)
    guess_v = (0.75 / h) * shift - 0.25 * (va + vb)
    if final is not None:
        guess_x = jnp.where(final, xa + h * va, guess_x)
        guess_v = jnp.where(final, va, guess_v)
    return wrapped(xo - guess_x), vo - guess_v


def updated(even, left, right):
    return tuple(e + 0.25 * (a + b) for e, a, b in zip(even, left, right))


def chosen(flag, a, b):
    return tuple(jnp.where(flag, p, q) for p, q in zip(a, b))


def kernel(
    counts_hbm, ids_hbm, traj, coef, oid,
    counts, ids, x, to_left, to_right, from_right, from_left, edge, edge_in, even, index, place, offs, *refs
):
    rows_of, xs, xr, zs, zr, u, w = (refs[4 * i : 4 * i + 4] for i in range(7))
    load_sem, far_sem, halo_s, halo_r, z_s, z_r, x_s, x_r = refs[28:]
    me = lax.axis_index("space")
    mx, mz = me // NZ, me % NZ
    mt = lax.axis_index("tm")
    first, final = mt == 0, mt == NT - 1
    left, right = (mt + NT - 1) % NT, (mt + 1) % NT

    def z_peer(k):
        z = (mz + k) % NZ
        return z, {"space": mx * NZ + z}

    def x_peer(k):
        xp = (mx + k) % NX
        return xp, {"space": xp * NZ + mz}

    barrier = pltpu.get_barrier_semaphore()
    peers = [z_peer(k)[1] for k in NEAR] + [x_peer(k)[1] for k in X_ORDER]
    peers += [{"tm": left}, {"tm": right}]
    for peer in peers:
        pl.semaphore_signal(barrier, inc=1, device_id=peer, device_id_type=MESH)

    loads = [
        pltpu.make_async_copy(counts_hbm, counts, load_sem.at[0]),
        pltpu.make_async_copy(traj, x, load_sem.at[1]),
        pltpu.make_async_copy(ids_hbm, ids, load_sem.at[2]),
    ]
    for load in loads:
        load.start()
    loads[0].wait()
    total = jnp.int32(0)
    for o in range(NX * NZ):
        offs[o] = total
        total = total + counts[0, o]

    lane = lax.broadcasted_iota(jnp.int32, (8, LANES), 1)
    row = lax.broadcasted_iota(jnp.int32, (8, LANES), 0)
    spare = lane >= SPAN

    for t in range(SLOT_TILES):
        base = t * LANES
        o0 = base // CAP
        shift, end = None, None
        for o in range(o0, (base + LANES - 1) // CAP + 1):
            begin = o * CAP - base
            shift_o, end_o = offs[o] - begin, begin + counts[0, o]
            if shift is None:
                shift, end = jnp.full((8, LANES), shift_o), jnp.full((8, LANES), end_o)
            else:
                shift, end = jnp.where(lane >= begin, shift_o, shift), jnp.where(lane >= begin, end_o, end)
        index[t] = jnp.where(lane < end, (lane + shift) & (LANES - 1), -1)
        start = offs[o0] + jnp.minimum(base - o0 * CAP, counts[0, o0])
        place[t] = (start >> 7) + (lane < (start & (LANES - 1))).astype(jnp.int32)

    loads[1].wait()
    loads[2].wait()

    def snap(i, lanes):
        return x[0:3, i, lanes], x[3:6, i, lanes]

    def pair(ref, i, lanes):
        return ref[6 * i : 6 * i + 3, lanes], ref[6 * i + 3 : 6 * i + 6, lanes]

    def put(ref, i, lanes, value):
        ref[6 * i : 6 * i + 3, lanes], ref[6 * i + 3 : 6 * i + 6, lanes] = value

    for c in range(ROWS // CHUNK):
        lanes = slice(c * CHUNK, (c + 1) * CHUNK)
        p = [snap(i, lanes) for i in range(8)]
        d1 = detail_of(p[0], p[1], p[2], 1.0)
        d3 = detail_of(p[2], p[3], p[4], 1.0)
        d5 = detail_of(p[4], p[5], p[6], 1.0)
        e2 = updated(p[2], d1, d3)
        e4 = updated(p[4], d3, d5)
        for i, v in enumerate((p[0], d1, e2, e4)):
            put(to_left, i, lanes, v)
        for i, v in enumerate((e4, d5, p[6], p[7])):
            put(to_right, i, lanes, v)
        for i, v in enumerate((d1, d3, d5)):
            put(rows_of[0], i, lanes, v)
        tag = (ids[0:1, lanes] + 1).astype(jnp.float32)
        rows_of[0][18:19, lanes] = tag
        rows_of[0][20:22, lanes] = d5[1][1:3]
        rows_of[0][22:23, lanes] = tag

    def spread(r, lanes, value):
        n = value.shape[0]
        i = 0
        while i < n:
            dst, at = rows_of[1 + (r + i) // 10], (r + i) % 10
            m = min(n - i, (8 if at < 8 else 10) - at)
            for again in range(1 if at < 8 else NX):
                dst[at + 2 * again : at + 2 * again + m, lanes] = value[i : i + m]
            i += m

    def pack(phase):
        src, dst = rows_of[phase], xs[phase]
        strips = PHASES[phase][0] // 8
        for t in range(SLOT_TILES):
            slots = index[t]
            live = slots >= 0
            slots = slots & (LANES - 1)
            where = place[t]
            low = max(0, (ROWS - (SLOT_TILES - t) * LANES) // LANES)
            high = min(t, ROWS // LANES - 1)
            lanes = slice((t % X_TILES) * LANES, (t % X_TILES + 1) * LANES)
            for strip in range(strips):
                rows = slice(8 * strip, 8 * strip + 8)
                block = src[rows, low * LANES : (low + 1) * LANES]
                for i in range(low + 1, high + 1):
                    block = jnp.where(where == i, src[rows, i * LANES : (i + 1) * LANES], block)
                taken = jnp.take_along_axis(block, slots, axis=1, mode="promise_in_bounds")
                dst[t // X_TILES, rows, lanes] = jnp.where(live, taken, 0.0)

    def remote(src, dst, send, recv, peer):
        return pltpu.make_async_remote_copy(
            src_ref=src, dst_ref=dst, send_sem=send, recv_sem=recv, device_id=peer, device_id_type=MESH
        )

    halos = [
        remote(to_left, from_right, halo_s.at[0], halo_r.at[0], {"tm": left}),
        remote(to_right, from_left, halo_s.at[1], halo_r.at[1], {"tm": right}),
        remote(edge, edge_in, halo_s.at[2], halo_r.at[2], {"tm": right}),
    ]

    def lanes_of(xp):
        return pl.ds(pl.multiple_of(xp * WIDE, LANES), WIDE)

    def x_refs(p, there, here):
        if p in Z_FIRST:
            return u[p].at[:, lanes_of(there)], w[p].at[:, lanes_of(here)]
        return xs[p].at[there], xr[p].at[here]

    def x_send(k, p):
        xp, peer = x_peer(k)
        src, dst = x_refs(p, xp, mx)
        return remote(src, dst, x_s.at[p, xp], x_r.at[p, mx], peer)

    def x_arrival(k, p):
        xp, peer = x_peer(k)
        src, dst = x_refs(p, xp, xp)
        return remote(src, dst, x_s.at[p, xp], x_r.at[p, xp], peer)

    def z_send(k, p):
        z, peer = z_peer(k)
        return remote(zs[p].at[z], zr[p].at[mz], z_s.at[p, z], z_r.at[p, mz], peer)

    def z_arrival(k, p):
        z, peer = z_peer(k)
        return remote(zs[p].at[z], zr[p].at[z], z_s.at[p, z], z_r.at[p, z], peer)

    def x_out(p):
        for k in X_ORDER:
            x_send(k, p).start()
        if p in Z_FIRST:
            w[p][:, lanes_of(mx)] = u[p][:, lanes_of(mx)]
        else:
            xr[p][mx] = xs[p][mx]

    def x_in(p):
        for k in X_ORDER:
            x_arrival(k, p).wait_recv()

    def z_out(p, order):
        for k in order:
            if p == 0 and k in FAR:
                if k <= NZ // 2:
                    pl.semaphore_wait(far_sem.at[k - REACH], 1)
                if k >= NZ // 2:
                    pl.semaphore_wait(far_sem.at[k + REACH], 1)
            z_send(k, p).start()

    def z_part(p, low, high, order=FAR_FIRST):
        for k in order:
            z = (mz + k) % NZ
            pl.when((z >= low) & (z < high))(lambda k=k: z_send(k, p).start())

    def z_in(p):
        for k in FAR_FIRST:
            z_arrival(k, p).wait_recv()

    def blocks_of(src, strip):
        rows = slice(8 * strip, 8 * strip + 8)
        return [
            [src[xp, rows, t * LANES : (t + 1) * LANES] for t in range(X_TILES)] for xp in range(NX)
        ]

    def piece(blocks, xp, z, lane_to):
        begin = z * CAP
        t = begin // LANES
        block = blocks[xp][t]
        if begin + CAP > (t + 1) * LANES:
            block = jnp.where(lane >= begin - t * LANES, block, blocks[xp][t + 1])
        turn = (lane_to - begin) % LANES
        return pltpu.roll(block, turn, 1) if turn else block

    def joined(blocks, z):
        out = piece(blocks, 0, z, 0)
        for xp in range(1, NX):
            out = jnp.where(lane >= xp * CAP, piece(blocks, xp, z, xp * CAP), out)
        return out

    def join(p, src):
        tiles = PHASES[p][1]
        per = NX // tiles
        last = blocks_of(src, tiles)
        for i in range(tiles):
            blocks = blocks_of(src, i)
            for z in range(NZ):
                more = piece(last, i, z, SPAN)
                for j in range(1, per):
                    more = jnp.where(row < 8 // per * j, more, piece(last, i + tiles * j, z, SPAN))
                zs[p][z, 8 * i : 8 * i + 8, :] = jnp.where(spare, more, joined(blocks, z))

    def own_z(p):
        zr[p][mz] = zs[p][mz]

    pack(0)
    join(0, xs[0])
    pl.semaphore_wait(barrier, len(peers))
    halos[0].start()
    halos[1].start()
    for k in NEAR:
        pl.semaphore_signal(far_sem.at[(NZ - k) % NZ], inc=1, device_id=z_peer(k)[1], device_id_type=MESH)


    z_out(0, NEAR)
    z_out(0, FAR[:6])

    halos[0].wait_recv()
    halos[1].wait_recv()

    for c in range(ROWS // CHUNK):
        lanes = slice(c * CHUNK, (c + 1) * CHUNK)
        x0, d1, e2, e4 = (pair(to_left, i, lanes) for i in range(4))
        d5, x6, x7 = (pair(to_right, i, lanes) for i in range(1, 4))
        x8, d9, e10, e12 = (pair(from_right, i, lanes) for i in range(4))
        em4, dm3, xm2, xm1 = (pair(from_left, i, lanes) for i in range(4))
        dm1 = detail_of(xm2, xm1, x0, 1.0)
        e0 = updated(x0, chosen(first, d1, dm1), d1)
        d7 = detail_of(x6, x7, x8, 1.0, final)
        e6 = updated(x6, d5, d7)
        e8 = updated(x8, d7, d9)
        em2 = updated(xm2, dm3, dm1)
        dm2 = detail_of(em4, em2, e0, 2.0)
        d2 = detail_of(e0, e2, e4, 2.0)
        d6 = detail_of(e4, e6, e8, 2.0, final)
        d10 = detail_of(e8, e10, e12, 2.0)
        f0 = updated(e0, chosen(first, d2, dm2), d2)
        f4 = updated(e4, d2, d6)
        f8 = updated(e8, d6, d10)
        d4 = detail_of(f0, f4, f8, 4.0, final)
        for i, v in enumerate((d7, d6, d2, d4)):
            spread(6 * i, lanes, v[0])
            spread(6 * i + 3, lanes, v[1])
        put(even, 0, lanes, f0)
        put(edge, 0, lanes, d4)

    halos[2].start()
    pack(2)
    x_out(2)
    z_out(0, FAR[6:])
    pack(1)
    join(1, xs[1])
    z_part(1, 0, 4)
    z_part(1, 4, 16)
    own_z(0)
    own_z(1)

    halos[2].wait_recv()
    d4 = edge[...]
    before = jnp.where(first, d4, edge_in[...])
    spread(24, slice(None), even[...] + 0.25 * (before + d4))
    pack(3)
    x_out(3)

    x_in(2)
    join(2, xr[2])
    z_part(2, 0, 4)
    own_z(2)
    x_in(3)
    join(3, xr[3])
    z_part(3, 0, 2)
    z_part(3, 2, 4)
    z_part(2, 4, 16, FAR_FIRST[:7])
    z_part(3, 4, 16, FAR_FIRST[:7])
    z_part(2, 4, 16, NEAR)
    z_part(3, 4, 16, NEAR)
    own_z(3)

    def unpack(dst, at, n, part):
        for xp in range(NX):
            tiles = [None] * X_TILES
            for z in range(NZ):
                block, begin, skip = part(z, xp)
                turn = (z * CAP - begin) % LANES
                turned = pltpu.roll(block, turn, 1) if turn else block
                for t in range(X_TILES):
                    low, high = z * CAP - t * LANES, (z + 1) * CAP - t * LANES
                    if high > 0 and low < LANES:
                        old = tiles[t]
                        tiles[t] = turned if old is None else jnp.where(lane >= low, turned, old)
            for t in range(X_TILES):
                lanes = slice((xp * X_TILES + t) * LANES, (xp * X_TILES + t + 1) * LANES)
                dst[at : at + n, lanes] = tiles[t][skip : skip + n]

    def unjoin(p, few):
        tiles = PHASES[p][1]
        per = NX // tiles
        for i in range(tiles):
            unpack(u[p], 8 * i, 8, lambda z, xp: (zr[p][z, 8 * i : 8 * i + 8, :], xp * CAP, 0))

        def rest(z, xp):
            i = xp % tiles
            return zr[p][z, 8 * i : 8 * i + 8, :], SPAN, 8 // per * (xp // tiles)

        unpack(u[p], 8 * tiles, few, rest)

    z_in(0)
    unjoin(0, 3)
    x_out(0)
    z_in(1)
    unjoin(1, 2)
    x_out(1)

    z_in(2)
    unjoin(2, 2)
    coef[4:6, 6, :] = u[2][0:2, :]
    coef[0:6, 2, :] = u[2][2:8, :]
    coef[0:2, 4, :] = u[2][8:10, :]
    x_in(0)
    coef[0:6, 1, :] = w[0][0:6, :]
    coef[0:6, 3, :] = w[0][6:12, :]
    coef[0:6, 5, :] = w[0][12:18, :]
    for t in range(SLOT_TILES):
        oid[t : t + 1, :] = w[0][18:19, t * LANES : (t + 1) * LANES].astype(jnp.int32) - 1
    x_in(1)
    coef[0:6, 7, :] = w[1][0:6, :]
    coef[0:4, 6, :] = w[1][6:10, :]

    z_in(3)
    unjoin(3, 2)
    coef[2:6, 4, :] = u[3][0:4, :]
    coef[0:6, 0, :] = u[3][4:10, :]

    for halo in halos:
        halo.wait_send()
    for p in range(len(PHASES)):
        for k in X_ORDER:
            x_send(k, p).wait_send()
        for k in FAR_FIRST:
            z_send(k, p).wait_send()


def per_device(trajectory, counts, particle_ids):
    f32, i32 = jnp.float32, jnp.int32
    vmem = lambda *shape: pltpu.VMEM(shape, f32)
    dma = pltpu.SemaphoreType.DMA
    slots = NX * WIDE
    coefficients, owned = pl.pallas_call(
        kernel,
        out_shape=(pltpu.VMEM((6, 8, slots), f32), pltpu.VMEM((SLOT_TILES, LANES), i32)),
        in_specs=[pl.BlockSpec(memory_space=pltpu.HBM)] * 3,
        out_specs=(pl.BlockSpec(memory_space=pltpu.VMEM), pl.BlockSpec(memory_space=pltpu.VMEM)),
        scratch_shapes=[
            pltpu.SMEM((1, NX * NZ), i32), pltpu.VMEM((1, ROWS), i32), vmem(6, 8, ROWS),
            vmem(24, ROWS), vmem(24, ROWS), vmem(24, ROWS), vmem(24, ROWS),
            vmem(6, ROWS), vmem(6, ROWS), vmem(6, ROWS),
            pltpu.VMEM((SLOT_TILES, 8, LANES), i32), pltpu.VMEM((SLOT_TILES, 8, LANES), i32),
            pltpu.SMEM((NX * NZ,), i32),
            *[vmem(rows, ROWS) for rows, _ in PHASES],
            *[vmem(NX, rows, WIDE) for rows, _ in PHASES],
            *[vmem(NX, rows, WIDE) for rows, _ in PHASES],
            *[vmem(NZ, 8 * tiles, LANES) for _, tiles in PHASES],
            *[vmem(NZ, 8 * tiles, LANES) for _, tiles in PHASES],
            *[vmem(rows, slots) for rows, _ in PHASES],
            *[vmem(rows, slots) for rows, _ in PHASES],
            dma((3,)), pltpu.SemaphoreType.REGULAR((NZ,)), dma((3,)), dma((3,)),
            dma((4, NZ)), dma((4, NZ)), dma((4, NX)), dma((4, NX)),
        ],
        compiler_params=pltpu.CompilerParams(
            collective_id=0, has_side_effects=True, vmem_limit_bytes=60 * 2**20
        ),
        name="regroup_and_lift",
    )(counts, particle_ids.reshape(1, ROWS), trajectory.transpose(1, 0, 2))
    return coefficients.transpose(1, 0, 2), owned.reshape(slots)


def solution(mesh):
    return jax.shard_map(
        per_device,
        mesh=mesh,
        in_specs=(P("tm", None, "space"), P("space", None), P("space")),
        out_specs=(P("tm", None, "space"), P("space")),
        check_vma=False,
    )
```

```python
import functools

import jax
import jax.numpy as jnp
from jax import lax
from jax.experimental import pallas as pl
from jax.experimental.pallas import tpu as pltpu
from jax.sharding import PartitionSpec as P

MESH = pl.DeviceIdType.MESH
NX = 4
NZ = 16
NT = 8
CAP = 24
ROWS = 1024
LANES = 128
SLOT_TILES = NX * NZ * CAP // LANES
WIDE = NZ * CAP
X_TILES = WIDE // LANES
CHUNK = 128
X_ORDER = (2, 1, 3)
REACH = 4
NEAR = (4, 12, 3, 13, 2, 14, 1, 15)
FAR = (5, 11, 6, 10, 7, 9, 8)
FAR_FIRST = (8, 7, 9, 6, 10, 5, 11) + NEAR
SPAN = NX * CAP
PHASES = ((24, 2), (16, 1), (16, 1), (16, 1))
Z_FIRST = (0, 1)


def wrapped(delta):
    return delta - 4.0 * jnp.floor(delta * 0.25 + 0.5)


def detail_of(start, odd, finish, h, final=None):
    (xa, va), (xo, vo), (xb, vb) = start, odd, finish
    shift = wrapped(xb - xa)
    guess_x = xa + 0.5 * shift + (0.25 * h) * (va - vb)
    guess_v = (0.75 / h) * shift - 0.25 * (va + vb)
    if final is not None:
        guess_x = jnp.where(final, xa + h * va, guess_x)
        guess_v = jnp.where(final, va, guess_v)
    return wrapped(xo - guess_x), vo - guess_v


def updated(even, left, right):
    return tuple(e + 0.25 * (a + b) for e, a, b in zip(even, left, right))


def chosen(flag, a, b):
    return tuple(jnp.where(flag, p, q) for p, q in zip(a, b))


def kernel(
    counts_hbm, ids_hbm, traj, coef, oid,
    counts, ids, x, to_left, to_right, from_right, from_left, edge, edge_in, even, index, place, offs, *refs
):
    rows_of, xs, xr, zs, zr, u, w = (refs[4 * i : 4 * i + 4] for i in range(7))
    load_sem, far_sem, halo_s, halo_r, z_s, z_r, x_s, x_r = refs[28:]
    me = lax.axis_index("space")
    mx, mz = me // NZ, me % NZ
    mt = lax.axis_index("tm")
    first, final = mt == 0, mt == NT - 1
    left, right = (mt + NT - 1) % NT, (mt + 1) % NT

    def z_peer(k):
        z = (mz + k) % NZ
        return z, {"space": mx * NZ + z}

    def x_peer(k):
        xp = (mx + k) % NX
        return xp, {"space": xp * NZ + mz}

    barrier = pltpu.get_barrier_semaphore()
    peers = [z_peer(k)[1] for k in NEAR] + [x_peer(k)[1] for k in X_ORDER]
    peers += [{"tm": left}, {"tm": right}]
    for peer in peers:
        pl.semaphore_signal(barrier, inc=1, device_id=peer, device_id_type=MESH)

    loads = [
        pltpu.make_async_copy(counts_hbm, counts, load_sem.at[0]),
        pltpu.make_async_copy(traj, x, load_sem.at[1]),
        pltpu.make_async_copy(ids_hbm, ids, load_sem.at[2]),
    ]
    for load in loads:
        load.start()
    loads[0].wait()
    total = jnp.int32(0)
    for o in range(NX * NZ):
        offs[o] = total
        total = total + counts[0, o]

    lane = lax.broadcasted_iota(jnp.int32, (8, LANES), 1)
    row = lax.broadcasted_iota(jnp.int32, (8, LANES), 0)
    spare = lane >= SPAN

    for t in range(SLOT_TILES):
        base = t * LANES
        o0 = base // CAP
        shift, end = None, None
        for o in range(o0, (base + LANES - 1) // CAP + 1):
            begin = o * CAP - base
            shift_o, end_o = offs[o] - begin, begin + counts[0, o]
            if shift is None:
                shift, end = jnp.full((8, LANES), shift_o), jnp.full((8, LANES), end_o)
            else:
                shift, end = jnp.where(lane >= begin, shift_o, shift), jnp.where(lane >= begin, end_o, end)
        index[t] = jnp.where(lane < end, (lane + shift) & (LANES - 1), -1)
        start = offs[o0] + jnp.minimum(base - o0 * CAP, counts[0, o0])
        place[t] = (start >> 7) + (lane < (start & (LANES - 1))).astype(jnp.int32)

    loads[1].wait()
    loads[2].wait()

    def snap(i, lanes):
        return x[0:3, i, lanes], x[3:6, i, lanes]

    def pair(ref, i, lanes):
        return ref[6 * i : 6 * i + 3, lanes], ref[6 * i + 3 : 6 * i + 6, lanes]

    def put(ref, i, lanes, value):
        ref[6 * i : 6 * i + 3, lanes], ref[6 * i + 3 : 6 * i + 6, lanes] = value

    for c in range(ROWS // CHUNK):
        lanes = slice(c * CHUNK, (c + 1) * CHUNK)
        p = [snap(i, lanes) for i in range(8)]
        d1 = detail_of(p[0], p[1], p[2], 1.0)
        d3 = detail_of(p[2], p[3], p[4], 1.0)
        d5 = detail_of(p[4], p[5], p[6], 1.0)
        e2 = updated(p[2], d1, d3)
        e4 = updated(p[4], d3, d5)
        for i, v in enumerate((p[0], d1, e2, e4)):
            put(to_left, i, lanes, v)
        for i, v in enumerate((e4, d5, p[6], p[7])):
            put(to_right, i, lanes, v)
        for i, v in enumerate((d1, d3, d5)):
            put(rows_of[0], i, lanes, v)
        tag = (ids[0:1, lanes] + 1).astype(jnp.float32)
        rows_of[0][18:19, lanes] = tag
        rows_of[0][20:22, lanes] = d5[1][1:3]
        rows_of[0][22:23, lanes] = tag

    def spread(r, lanes, value):
        n = value.shape[0]
        i = 0
        while i < n:
            dst, at = rows_of[1 + (r + i) // 10], (r + i) % 10
            m = min(n - i, (8 if at < 8 else 10) - at)
            for again in range(1 if at < 8 else NX):
                dst[at + 2 * again : at + 2 * again + m, lanes] = value[i : i + m]
            i += m

    def pack(phase):
        src, dst = rows_of[phase], xs[phase]
        strips = PHASES[phase][0] // 8
        for t in range(SLOT_TILES):
            slots = index[t]
            live = slots >= 0
            slots = slots & (LANES - 1)
            where = place[t]
            low = max(0, (ROWS - (SLOT_TILES - t) * LANES) // LANES)
            high = min(t, ROWS // LANES - 1)
            lanes = slice((t % X_TILES) * LANES, (t % X_TILES + 1) * LANES)
            for strip in range(strips):
                rows = slice(8 * strip, 8 * strip + 8)
                block = src[rows, low * LANES : (low + 1) * LANES]
                for i in range(low + 1, high + 1):
                    block = jnp.where(where == i, src[rows, i * LANES : (i + 1) * LANES], block)
                taken = jnp.take_along_axis(block, slots, axis=1, mode="promise_in_bounds")
                dst[t // X_TILES, rows, lanes] = jnp.where(live, taken, 0.0)

    def remote(src, dst, send, recv, peer):
        return pltpu.make_async_remote_copy(
            src_ref=src, dst_ref=dst, send_sem=send, recv_sem=recv, device_id=peer, device_id_type=MESH
        )

    halos = [
        remote(to_left, from_right, halo_s.at[0], halo_r.at[0], {"tm": left}),
        remote(to_right, from_left, halo_s.at[1], halo_r.at[1], {"tm": right}),
        remote(edge, edge_in, halo_s.at[2], halo_r.at[2], {"tm": right}),
    ]

    def lanes_of(xp):
        return pl.ds(pl.multiple_of(xp * WIDE, LANES), WIDE)

    def x_refs(p, there, here):
        if p in Z_FIRST:
            return u[p].at[:, lanes_of(there)], w[p].at[:, lanes_of(here)]
        return xs[p].at[there], xr[p].at[here]

    def x_send(k, p):
        xp, peer = x_peer(k)
        src, dst = x_refs(p, xp, mx)
        return remote(src, dst, x_s.at[p, xp], x_r.at[p, mx], peer)

    def x_arrival(k, p):
        xp, peer = x_peer(k)
        src, dst = x_refs(p, xp, xp)
        return remote(src, dst, x_s.at[p, xp], x_r.at[p, xp], peer)

    def z_send(k, p):
        z, peer = z_peer(k)
        return remote(zs[p].at[z], zr[p].at[mz], z_s.at[p, z], z_r.at[p, mz], peer)

    def z_arrival(k, p):
        z, peer = z_peer(k)
        return remote(zs[p].at[z], zr[p].at[z], z_s.at[p, z], z_r.at[p, z], peer)

    def x_out(p):
        for k in X_ORDER:
            x_send(k, p).start()
        if p in Z_FIRST:
            w[p][:, lanes_of(mx)] = u[p][:, lanes_of(mx)]
        else:
            xr[p][mx] = xs[p][mx]

    def x_in(p):
        for k in X_ORDER:
            x_arrival(k, p).wait_recv()

    def z_out(p, order):
        for k in order:
            if p == 0 and k in FAR:
                if k <= NZ // 2:
                    pl.semaphore_wait(far_sem.at[k - REACH], 1)
                if k >= NZ // 2:
                    pl.semaphore_wait(far_sem.at[k + REACH], 1)
            z_send(k, p).start()

    def z_part(p, low, high, order=FAR_FIRST):
        for k in order:
            z = (mz + k) % NZ
            pl.when((z >= low) & (z < high))(lambda k=k: z_send(k, p).start())

    def z_in(p):
        for k in FAR_FIRST:
            z_arrival(k, p).wait_recv()

    def blocks_of(src, strip):
        rows = slice(8 * strip, 8 * strip + 8)
        return [
            [src[xp, rows, t * LANES : (t + 1) * LANES] for t in range(X_TILES)] for xp in range(NX)
        ]

    def piece(blocks, xp, z, lane_to):
        begin = z * CAP
        t = begin // LANES
        block = blocks[xp][t]
        if begin + CAP > (t + 1) * LANES:
            block = jnp.where(lane >= begin - t * LANES, block, blocks[xp][t + 1])
        turn = (lane_to - begin) % LANES
        return pltpu.roll(block, turn, 1) if turn else block

    def joined(blocks, z):
        out = piece(blocks, 0, z, 0)
        for xp in range(1, NX):
            out = jnp.where(lane >= xp * CAP, piece(blocks, xp, z, xp * CAP), out)
        return out

    def join(p, src):
        tiles = PHASES[p][1]
        per = NX // tiles
        last = blocks_of(src, tiles)
        for i in range(tiles):
            blocks = blocks_of(src, i)
            for z in range(NZ):
                more = piece(last, i, z, SPAN)
                for j in range(1, per):
                    more = jnp.where(row < 8 // per * j, more, piece(last, i + tiles * j, z, SPAN))
                zs[p][z, 8 * i : 8 * i + 8, :] = jnp.where(spare, more, joined(blocks, z))

    def own_z(p):
        zr[p][mz] = zs[p][mz]

    pack(0)
    join(0, xs[0])
    pl.semaphore_wait(barrier, len(peers))
    halos[0].start()
    halos[1].start()
    for k in NEAR:
        pl.semaphore_signal(far_sem.at[(NZ - k) % NZ], inc=1, device_id=z_peer(k)[1], device_id_type=MESH)


    z_out(0, NEAR)
    z_out(0, FAR[:6])

    halos[0].wait_recv()
    halos[1].wait_recv()

    for c in range(ROWS // CHUNK):
        lanes = slice(c * CHUNK, (c + 1) * CHUNK)
        x0, d1, e2, e4 = (pair(to_left, i, lanes) for i in range(4))
        d5, x6, x7 = (pair(to_right, i, lanes) for i in range(1, 4))
        x8, d9, e10, e12 = (pair(from_right, i, lanes) for i in range(4))
        em4, dm3, xm2, xm1 = (pair(from_left, i, lanes) for i in range(4))
        dm1 = detail_of(xm2, xm1, x0, 1.0)
        e0 = updated(x0, chosen(first, d1, dm1), d1)
        d7 = detail_of(x6, x7, x8, 1.0, final)
        e6 = updated(x6, d5, d7)
        e8 = updated(x8, d7, d9)
        em2 = updated(xm2, dm3, dm1)
        dm2 = detail_of(em4, em2, e0, 2.0)
        d2 = detail_of(e0, e2, e4, 2.0)
        d6 = detail_of(e4, e6, e8, 2.0, final)
        d10 = detail_of(e8, e10, e12, 2.0)
        f0 = updated(e0, chosen(first, d2, dm2), d2)
        f4 = updated(e4, d2, d6)
        f8 = updated(e8, d6, d10)
        d4 = detail_of(f0, f4, f8, 4.0, final)
        for i, v in enumerate((d7, d6, d2, d4)):
            spread(6 * i, lanes, v[0])
            spread(6 * i + 3, lanes, v[1])
        put(even, 0, lanes, f0)
        put(edge, 0, lanes, d4)

    halos[2].start()
    pack(2)
    x_out(2)
    z_out(0, FAR[6:])
    pack(1)
    join(1, xs[1])
    z_part(1, 0, 4)
    z_part(1, 4, 16)
    own_z(0)
    own_z(1)

    halos[2].wait_recv()
    d4 = edge[...]
    before = jnp.where(first, d4, edge_in[...])
    spread(24, slice(None), even[...] + 0.25 * (before + d4))
    pack(3)
    x_out(3)

    x_in(2)
    join(2, xr[2])
    z_part(2, 0, 4)
    own_z(2)
    x_in(3)
    join(3, xr[3])
    z_part(3, 0, 2)
    z_part(3, 2, 4)
    z_part(2, 4, 16, FAR_FIRST[:7])
    z_part(3, 4, 16, FAR_FIRST[:7])
    z_part(2, 4, 16, NEAR)
    z_part(3, 4, 16, NEAR)
    own_z(3)

    def unpack(dst, at, n, part):
        for xp in range(NX):
            tiles = [None] * X_TILES
            for z in range(NZ):
                block, begin, skip = part(z, xp)
                turn = (z * CAP - begin) % LANES
                turned = pltpu.roll(block, turn, 1) if turn else block
                for t in range(X_TILES):
                    low, high = z * CAP - t * LANES, (z + 1) * CAP - t * LANES
                    if high > 0 and low < LANES:
                        old = tiles[t]
                        tiles[t] = turned if old is None else jnp.where(lane >= low, turned, old)
            for t in range(X_TILES):
                lanes = slice((xp * X_TILES + t) * LANES, (xp * X_TILES + t + 1) * LANES)
                dst[at : at + n, lanes] = tiles[t][skip : skip + n]

    def unjoin(p, few):
        tiles = PHASES[p][1]
        per = NX // tiles
        for i in range(tiles):
            unpack(u[p], 8 * i, 8, lambda z, xp: (zr[p][z, 8 * i : 8 * i + 8, :], xp * CAP, 0))

        def rest(z, xp):
            i = xp % tiles
            return zr[p][z, 8 * i : 8 * i + 8, :], SPAN, 8 // per * (xp // tiles)

        unpack(u[p], 8 * tiles, few, rest)

    z_in(0)
    unjoin(0, 3)
    x_out(0)
    z_in(1)
    unjoin(1, 2)
    x_out(1)

    z_in(2)
    unjoin(2, 2)
    coef[4:6, 6, :] = u[2][0:2, :]
    coef[0:6, 2, :] = u[2][2:8, :]
    coef[0:2, 4, :] = u[2][8:10, :]
    x_in(0)
    coef[0:6, 1, :] = w[0][0:6, :]
    coef[0:6, 3, :] = w[0][6:12, :]
    coef[0:6, 5, :] = w[0][12:18, :]
    for t in range(SLOT_TILES):
        oid[t : t + 1, :] = w[0][18:19, t * LANES : (t + 1) * LANES].astype(jnp.int32) - 1
    x_in(1)
    coef[0:6, 7, :] = w[1][0:6, :]
    coef[0:4, 6, :] = w[1][6:10, :]

    z_in(3)
    unjoin(3, 2)
    coef[2:6, 4, :] = u[3][0:4, :]
    coef[0:6, 0, :] = u[3][4:10, :]

    for halo in halos:
        halo.wait_send()
    for p in range(len(PHASES)):
        for k in X_ORDER:
            x_send(k, p).wait_send()
        for k in FAR_FIRST:
            z_send(k, p).wait_send()


def per_device(trajectory, counts, particle_ids):
    f32, i32 = jnp.float32, jnp.int32
    vmem = lambda *shape: pltpu.VMEM(shape, f32)
    dma = pltpu.SemaphoreType.DMA
    slots = NX * WIDE
    coefficients, owned = pl.pallas_call(
        kernel,
        out_shape=(pltpu.VMEM((6, 8, slots), f32), pltpu.VMEM((SLOT_TILES, LANES), i32)),
        in_specs=[pl.BlockSpec(memory_space=pltpu.HBM)] * 3,
        out_specs=(pl.BlockSpec(memory_space=pltpu.VMEM), pl.BlockSpec(memory_space=pltpu.VMEM)),
        scratch_shapes=[
            pltpu.SMEM((1, NX * NZ), i32), pltpu.VMEM((1, ROWS), i32), vmem(6, 8, ROWS),
            vmem(24, ROWS), vmem(24, ROWS), vmem(24, ROWS), vmem(24, ROWS),
            vmem(6, ROWS), vmem(6, ROWS), vmem(6, ROWS),
            pltpu.VMEM((SLOT_TILES, 8, LANES), i32), pltpu.VMEM((SLOT_TILES, 8, LANES), i32),
            pltpu.SMEM((NX * NZ,), i32),
            *[vmem(rows, ROWS) for rows, _ in PHASES],
            *[vmem(NX, rows, WIDE) for rows, _ in PHASES],
            *[vmem(NX, rows, WIDE) for rows, _ in PHASES],
            *[vmem(NZ, 8 * tiles, LANES) for _, tiles in PHASES],
            *[vmem(NZ, 8 * tiles, LANES) for _, tiles in PHASES],
            *[vmem(rows, slots) for rows, _ in PHASES],
            *[vmem(rows, slots) for rows, _ in PHASES],
            dma((3,)), pltpu.SemaphoreType.REGULAR((NZ,)), dma((3,)), dma((3,)),
            dma((4, NZ)), dma((4, NZ)), dma((4, NX)), dma((4, NX)),
        ],
        compiler_params=pltpu.CompilerParams(
            collective_id=0, has_side_effects=True, vmem_limit_bytes=60 * 2**20
        ),
        name="regroup_and_lift",
    )(counts, particle_ids.reshape(1, ROWS), trajectory.transpose(1, 0, 2))
    return coefficients.transpose(1, 0, 2), owned.reshape(slots)


def solution(mesh):
    return jax.shard_map(
        per_device,
        mesh=mesh,
        in_specs=(P("tm", None, "space"), P("space", None), P("space")),
        out_specs=(P("tm", None, "space"), P("space")),
        check_vma=False,
    )
```
